128 devices in a mesh: row: 16 (over z_lo, x, core), col: 8 (over y, z_hi).
Axes of the slice: x: 4, y: 4, z: 4 (z_hi: 2, z_lo: 2; z = z_hi * 2 + z_lo), core: 2. Of those that a mesh axis runs over, the one named last changes fastest.
Arguments:
- grad: float32 [5120, 8192], P('row', 'col'), may hold values from -180 to 180
- momentum: float32 [5120, 8192], P('row', 'col'), may hold values from -30 to 30
Outputs:
- update: bfloat16 [5120, 8192], P('row', 'col')
- new_momentum: float32 [5120, 8192], P('row', 'col')
The draws below stay inside these ranges and needn't reach their ends.
All inputs are finite; a program needn't handle non-finite values.
Results may differ from the reference program's by a relative error of at most 0.0013.
The reference program's roundings to bfloat16 on the way count: a program that leaves them out, or rounds other values in their place, can miss the bound.
Values may be sent and summed in bfloat16 or wider, within the bound.
A program may use at most 128 MiB of HBM per device.

```python
import math
import jax
import jax.numpy as jnp

M = 5120
N = 8192


def draw_grad(key, part):
    key = jax.random.fold_in(key, 17)
    subkeys = jax.random.split(key, 3)
    row_place = jnp.arange(M, dtype=jnp.float32) / M
    col_place = jnp.arange(N, dtype=jnp.float32) / N
    spread = math.log(10.0)
    noise_field = jnp.clip(jax.random.normal(subkeys[0], (M, N), jnp.float32), -6.0, 6.0)
    row_scale = jnp.exp(0.5 * math.log(3.0) * row_place + 0.5 * spread * jax.random.uniform(subkeys[1], (M,), jnp.float32))
    col_scale = jnp.exp(0.5 * math.log(3.0) * col_place + 0.5 * spread * jax.random.uniform(subkeys[2], (N,), jnp.float32))
    return noise_field * row_scale[:, None] * col_scale[None, :]


def block_levels(stream_key, dims, cuts, low, top_value):
    def one(axis_at, blocks):
        draws = jax.random.uniform(jax.random.fold_in(jax.random.fold_in(stream_key, 6), axis_at), (blocks,), jnp.float32, low / len(cuts), top_value / len(cuts))
        return jnp.repeat(jnp.exp(draws), dims[axis_at] // blocks).reshape((-1,) + (1,) * (len(dims) - axis_at - 1))

    level = one(*cuts[0])
    for cut in cuts[1:]:
        level = level * one(*cut)
    return level


def normal_values(rng, dims, scale, most, pieces=(), held_as=jnp.bfloat16):
    gain = block_levels(rng, dims, pieces, -0.22, 0.18) if pieces else 1.0
    array = jax.random.normal(rng, dims, jnp.float32) * scale * gain
    return jnp.minimum(jnp.maximum(array, -most), most).astype(held_as)


def setup_inputs(seed: int = 0) -> dict:
    seeds = jax.random.split(jax.random.key(seed), 3)
    grad = draw_grad(jax.random.fold_in(seeds[2], 71), 0)
    momentum = normal_values(seeds[1], (M, N), 5.0, 30.0, ((0, 16), (1, 8)), jnp.float32)
    return dict(grad=grad, momentum=momentum)


momentum_decay = 0.95
target_rms = 0.25
norm_epsilon = 1e-07
coef_linear = 3.4445
coef_cubic = -4.775
coef_quintic = 2.0315

def reference(grad, momentum):
    new_momentum = momentum_decay * momentum + grad
    blended = (grad + momentum_decay * new_momentum).astype(jnp.bfloat16)
    blended_wide = blended.astype(jnp.float32)
    squares_total = jnp.sum(blended_wide * blended_wide)
    norm_scale = target_rms * math.sqrt(M) / (jnp.sqrt(squares_total) + norm_epsilon)
    ortho_matrix = (blended_wide * norm_scale).astype(jnp.bfloat16)
    gram_matrix = jnp.dot(ortho_matrix, ortho_matrix.T, preferred_element_type=jnp.float32).astype(jnp.bfloat16)
    square = jnp.dot(gram_matrix, gram_matrix, preferred_element_type=jnp.float32)
    polynomial = (coef_cubic * gram_matrix.astype(jnp.float32) + coef_quintic * square).astype(jnp.bfloat16)
    product = jnp.dot(polynomial, ortho_matrix, preferred_element_type=jnp.float32)
    update = (math.sqrt(N) * (coef_linear * ortho_matrix.astype(jnp.float32) + product)).astype(jnp.bfloat16)
    return (update, new_momentum)
```

```python
import math

import jax
import jax.numpy as jnp
from jax import lax
from jax.sharding import PartitionSpec as P

momentum_decay = 0.95
target_rms = 0.25
norm_epsilon = 1e-07
coef_linear = 3.4445
coef_cubic = -4.775
coef_quintic = 2.0315


def per_device(grad, momentum):
    tile_rows, tile_cols = grad.shape
    row_devices = lax.axis_size("row")
    col_devices = lax.axis_size("col")
    total_rows = tile_rows * row_devices
    total_cols = tile_cols * col_devices
    new_momentum = momentum_decay * momentum + grad
    blended = (grad + momentum_decay * new_momentum).astype(jnp.bfloat16)
    column = lax.all_gather(blended, "row", axis=0, tiled=True)
    tile_wide = blended.astype(jnp.float32)
    squares_total = lax.psum(jnp.sum(tile_wide * tile_wide), ("row", "col"))
    norm_scale = target_rms * math.sqrt(total_rows) / (jnp.sqrt(squares_total) + norm_epsilon)
    ortho_column = (column.astype(jnp.float32) * norm_scale).astype(jnp.bfloat16)
    ortho_tile = lax.dynamic_slice_in_dim(
        ortho_column, lax.axis_index("row") * tile_rows, tile_rows, 0
    )
    gram_mirror = lax.psum_scatter(
        lax.dot_general(
            ortho_column, ortho_tile, (((1,), (1,)), ((), ())), preferred_element_type=jnp.float32
        ),
        "col",
        scatter_dimension=0,
        tiled=True,
    )
    gram_tile = gram_mirror.T.astype(jnp.bfloat16)
    gram_rows = lax.all_gather(gram_tile, "col", axis=1, tiled=True)
    gram_cols = lax.all_gather(gram_tile, "row", axis=0, tiled=True)
    square = jnp.dot(gram_rows, gram_cols, preferred_element_type=jnp.float32)
    poly_tile = (coef_cubic * gram_tile.astype(jnp.float32) + coef_quintic * square).astype(
        jnp.bfloat16
    )
    poly_rows = lax.all_gather(poly_tile, "col", axis=1, tiled=True)
    product = jnp.dot(poly_rows, ortho_column, preferred_element_type=jnp.float32)
    update = (
        math.sqrt(total_cols) * (coef_linear * ortho_tile.astype(jnp.float32) + product)
    ).astype(jnp.bfloat16)
    return (update, new_momentum)


def solution(mesh):
    placed = (P("row", "col"), P("row", "col"))
    return jax.shard_map(
        per_device,
        mesh=mesh,
        in_specs=placed,
        out_specs=(P("row", "col"), P("row", "col")),
        check_vma=False,
    )
```

```python
import math

import jax
import jax.numpy as jnp
from jax import lax
from jax.experimental import pallas as pl
from jax.experimental.pallas import tpu as pltpu
from jax.sharding import PartitionSpec as P

momentum_decay = 0.95
target_rms = 0.25
norm_epsilon = 1e-07
coef_linear = 3.4445
coef_cubic = -4.775
coef_quintic = 2.0315

MESH = pl.DeviceIdType.MESH
F32 = jnp.float32
BF16 = jnp.bfloat16

TILE = 320
BLOCK = 640
WIDTH = 1024
PIECE = 80


class Gather:
    def __init__(self, own, whole, half, p, b, right, left, pair, send, recv):
        def copy(n, src, dst, device):
            return pltpu.make_async_remote_copy(
                src, dst, send.at[n], recv.at[n], device_id=device, device_id_type=MESH
            )

        lo, hi = lax.rem(p + 3, 4), lax.rem(p + 1, 4)
        c = 1 - b
        own_place = whole(p, b)
        self.pair = copy(0, own, own_place, pair)
        self.right = copy(1, own, own_place, right)
        self.left = copy(2, own, own_place, left)
        self.right_pair = copy(3, whole(p, c), whole(p, c), right)
        self.left_pair = copy(4, whole(p, c), whole(p, c), left)
        self.on_right = copy(5, half(lo, b, 0), half(lo, b, 0), right)
        self.on_left = copy(6, half(hi, b, 1), half(hi, b, 1), left)
        self.on_right_pair = copy(7, half(lo, c, 0), half(lo, c, 0), right)
        self.on_left_pair = copy(8, half(hi, c, 1), half(hi, c, 1), left)
        opp = lax.rem(p + 2, 4)
        self.order = [(p, b), (p, c), (lo, b), (hi, b), (lo, c), (hi, c), (opp, b), (opp, c)]

    def start(self):
        self.pair.start()
        self.right.start()
        self.left.start()

    def arrive(self, n):
        if n == 1:
            self.pair.wait_recv()
            self.right_pair.start()
            self.left_pair.start()
        elif n == 2:
            self.right.wait_recv()
            self.on_right.start()
        elif n == 3:
            self.left.wait_recv()
            self.on_left.start()
        elif n == 4:
            self.right_pair.wait_recv()
            self.on_right_pair.start()
        elif n == 5:
            self.left_pair.wait_recv()
            self.on_left_pair.start()
        elif n == 6:
            self.on_right.wait_recv()
            self.on_left.wait_recv()
        elif n == 7:
            self.on_right_pair.wait_recv()
            self.on_left_pair.wait_recv()

    def finish(self):
        for c in (
            self.pair, self.right, self.left, self.right_pair, self.left_pair,
            self.on_right, self.on_left, self.on_right_pair, self.on_left_pair,
        ):
            c.wait_send()


def kernel(
    blended, out,
    raw, ortho, part, hop_half, hop_whole, hop_pair, gram_cols, gram_rows, poly, square, total, sums,
    b_send, b_recv, bs_send, bs_recv, half_send, half_recv, whole_send, whole_recv, z_send, z_recv,
    gr_send, gr_recv, gc_send, gc_recv, gs_send, gs_recv, p_send, p_recv, ps_send, ps_recv,
    sum_send, sum_recv,
):
    row, col = lax.axis_index("row"), lax.axis_index("col")
    core = lax.rem(row, 2)
    x = lax.rem(lax.div(row, 2), 4)
    z_lo = lax.div(row, 8)
    y, z_hi = lax.div(col, 2), lax.rem(col, 2)
    chip_row = lax.div(row, 2)

    def at(x=x, y=y, z_lo=z_lo, z_hi=z_hi, core=core):
        return ((z_lo * 4 + x) * 2 + core, y * 2 + z_hi)

    def turn(v, n):
        return lax.rem(v + n, 4)

    sibling = at(core=1 - core)
    x_right, x_left = at(x=turn(x, 1)), at(x=turn(x, 3))
    y_right, y_left = at(y=turn(y, 1)), at(y=turn(y, 3))
    lo_pair, hi_pair = at(z_lo=1 - z_lo), at(z_hi=1 - z_hi)
    z = z_hi * 2 + z_lo
    peers = {
        "core": [sibling],
        "x": [at(x=turn(x, n)) for n in (1, 2, 3)],
        "y": [at(y=turn(y, n)) for n in (1, 2, 3)],
        "z": [at(z_lo=lax.rem(turn(z, n), 2), z_hi=lax.div(turn(z, n), 2)) for n in (1, 2, 3)],
    }
    everyone = [d for group in peers.values() for d in group]

    barrier = pltpu.get_barrier_semaphore()
    for d in everyone:
        pl.semaphore_signal(barrier, inc=1, device_id=d, device_id_type=MESH)
    pl.semaphore_wait(barrier, len(everyone))

    gather_b = Gather(
        blended,
        lambda p, b: raw.at[b * 4 + p],
        lambda p, b, k: raw.at[b * 4 + p, pl.ds(k * 160, 160)],
        x, z_lo, x_right, x_left, lo_pair, b_send, b_recv,
    )
    gather_b.start()

    mine = jnp.zeros((8, 128), F32)
    for k in range(8):
        wide = blended[:, k * 128 : (k + 1) * 128].astype(F32).reshape(TILE // 8, 8, 128)
        mine = mine + jnp.sum(wide * wide, axis=0)
    for stage, (place, size) in enumerate(((core, 2), (x, 4), (y, 4), (z, 4))):
        group = list(peers.values())[stage]
        sums[stage, place] = mine
        copies = [
            pltpu.make_async_remote_copy(
                sums.at[stage, place], sums.at[stage, place],
                sum_send.at[stage, n], sum_recv.at[stage, n], device_id=d, device_id_type=MESH,
            )
            for n, d in enumerate(group)
        ]
        for c in copies:
            c.start()
        for c in copies:
            c.wait()
        mine = sums[stage, 0]
        for n in range(1, size):
            mine = mine + sums[stage, n]
    squares_total = jnp.sum(mine, keepdims=True)
    norm_scale = target_rms * math.sqrt(5120) / (jnp.sqrt(squares_total) + norm_epsilon)

    def to_sibling(n, src, send, recv):
        return pltpu.make_async_remote_copy(
            src, src, send.at[n], recv.at[n], device_id=sibling, device_id_type=MESH
        )

    mine_rows = pl.ds(pl.multiple_of(y * PIECE, PIECE), PIECE)

    def scale(src, j):
        def body(k, carry):
            rows = pl.ds(pl.multiple_of(k * 32, 32), 32)
            ortho[j, core, rows] = (src[rows].astype(F32) * norm_scale).astype(BF16)
            return carry

        lax.fori_loop(0, TILE // 32, body, 0)

    def partial(p, b):
        part[b, p] = lax.dot_general(
            ortho[b * 4 + p, core],
            ortho[chip_row].reshape(BLOCK, WIDTH),
            (((1,), (1,)), ((), ())),
            preferred_element_type=F32,
        )

    def half_hops(n, p, b):
        far = turn(y, 2) * PIECE
        return [
            pltpu.make_async_remote_copy(
                part.at[b, p, pl.ds(pl.multiple_of(far + 40 * k, 8), 40)],
                hop_half.at[n, k],
                half_send.at[n, k], half_recv.at[n, k], device_id=d, device_id_type=MESH,
            )
            for k, d in enumerate((y_right, y_left))
        ]

    def whole_hops(n, p, b):
        return [
            pltpu.make_async_remote_copy(
                part.at[b, p, pl.ds(pl.multiple_of(near * PIECE, 8), PIECE)],
                hop_whole.at[n, k],
                whole_send.at[n, k], whole_recv.at[n, k], device_id=d, device_id_type=MESH,
            )
            for k, (near, d) in enumerate(((turn(y, 1), y_right), (turn(y, 3), y_left)))
        ]

    def pair_hop(n, p):
        return pltpu.make_async_remote_copy(
            part.at[1 - z_hi, p, mine_rows], hop_pair.at[n],
            z_send.at[n], z_recv.at[n], device_id=hi_pair, device_id_type=MESH,
        )

    order = gather_b.order

    def reduce_1(n):
        for c in half_hops(n, *order[n]):
            c.start()

    def reduce_2(n):
        p, b = order[n]
        halves, wholes = half_hops(n, p, b), whole_hops(n, p, b)
        for k, near in enumerate((turn(y, 1), turn(y, 3))):
            halves[k].wait_recv()
            rows = pl.ds(pl.multiple_of(near * PIECE + 40 * k, 8), 40)
            part[b, p, rows] = part[b, p, rows] + hop_half[n, k]
            wholes[k].start()

    def reduce_3(n):
        p, b = order[n]
        for c in whole_hops(n, p, b):
            c.wait_recv()
        part[b, p, mine_rows] = part[b, p, mine_rows] + (hop_whole[n, 0] + hop_whole[n, 1])

    twos = ((0, 1), (2, 4), (3, 5), (6, 7))

    def reduce_4(m):
        pair_hop(m, order[twos[m][0]][0]).start()

    def reduce_5(m):
        p = order[twos[m][0]][0]
        pair_hop(m, p).wait_recv()
        tile = (part[z_hi, p, mine_rows] + hop_pair[m]).astype(BF16)
        gram_cols[z_hi, p, core, y] = tile
        gram_rows[chip_row, pl.ds(pl.multiple_of(p * PIECE, 16), PIECE)] = tile

    def own_block():
        scale(blended, chip_row)
        to_sibling(0, ortho.at[chip_row, core], bs_send, bs_recv).start()
        to_sibling(0, ortho.at[chip_row, core], bs_send, bs_recv).wait_recv()

    for n in range(11):
        if n < 8:
            p, b = order[n]
            gather_b.arrive(n)
            if n == 0:
                own_block()
            else:
                scale(raw.at[b * 4 + p], b * 4 + p)
                to_sibling(n, ortho.at[b * 4 + p, core], bs_send, bs_recv).start()
            partial(p, b)
            reduce_1(n)
        if 1 <= n < 9:
            reduce_2(n - 1)
        if 2 <= n < 10:
            reduce_3(n - 2)
            for m, (_, second) in enumerate(twos):
                if second == n - 2:
                    reduce_4(m)
        if 3 <= n:
            for m, (_, second) in enumerate(twos):
                if second == n - 3:
                    reduce_5(m)

    def rows_half(p, b, k):
        return gram_rows.at[b * 4 + p, pl.ds(k * 160, 160)]

    gather_rows = Gather(
        gram_rows.at[chip_row], lambda p, b: gram_rows.at[b * 4 + p], rows_half,
        x, z_lo, x_right, x_left, lo_pair, gr_send, gr_recv,
    )
    gather_cols = Gather(
        gram_cols.at[z_hi, :, core, y],
        lambda p, b: gram_cols.at[b, :, core, p],
        lambda p, b, k: gram_cols.at[b, pl.ds(k * 2, 2), core, p],
        y, z_hi, y_right, y_left, hi_pair, gc_send, gc_recv,
    )
    gather_cols.start()
    gather_rows.start()

    def cols_to_sibling(n):
        p, b = gather_cols.order[n]
        return to_sibling(n, gram_cols.at[b, :, core, p], gs_send, gs_recv)

    for n in range(8):
        gather_cols.arrive(n)
        cols_to_sibling(n).start()
        gather_rows.arrive(n)
    for n in range(8):
        cols_to_sibling(n).wait_recv()

    square[...] = jnp.zeros_like(square)

    def add_square(k, carry):
        right = gram_cols[lax.div(k, 4), lax.rem(k, 4)].reshape(BLOCK, BLOCK)
        square[...] += jnp.dot(gram_rows[k], right, preferred_element_type=F32)
        return carry

    lax.fori_loop(0, 8, add_square, 0)
    poly[col, core] = (
        coef_cubic * gram_rows[chip_row].astype(F32) + coef_quintic * square[...]
    ).astype(BF16)

    gather_p = Gather(
        poly.at[col, core],
        lambda p, b: poly.at[p * 2 + b, core],
        lambda p, b, k: poly.at[p * 2 + b, core, pl.ds(k * 160, 160)],
        y, z_hi, y_right, y_left, hi_pair, p_send, p_recv,
    )
    gather_p.start()

    def poly_to_sibling(n):
        p, b = gather_p.order[n]
        return to_sibling(n, poly.at[p * 2 + b, core], ps_send, ps_recv)

    for n in range(1, 8):
        p, b = order[n]
        to_sibling(n, ortho.at[b * 4 + p, core], bs_send, bs_recv).wait_recv()

    lanes = pl.ds(pl.multiple_of(core * 256, 128), 384)
    total[...] = jnp.zeros_like(total)

    def add_product(p, b):
        def body(a, carry):
            left = poly[p * 2 + b, a, :, lanes]
            first = pl.multiple_of(p * PIECE, 16)
            right = jnp.concatenate(
                [ortho[b * 4 + k, a, pl.ds(first, PIECE)] for k in range(4)], axis=0
            )
            total[...] += lax.dot_general(
                left, right, (((0,), (0,)), ((), ())), preferred_element_type=F32
            )
            return carry

        lax.fori_loop(0, 2, body, 0)

    for n in range(8):
        gather_p.arrive(n)
        poly_to_sibling(n).start()
        poly_to_sibling(n).wait_recv()
        add_product(*gather_p.order[n])

    product = total[pl.ds(pl.multiple_of(core * 64, 8), TILE)]
    out[...] = (
        math.sqrt(8192) * (coef_linear * ortho[chip_row, core].astype(F32) + product)
    ).astype(BF16)

    for g in (gather_b, gather_rows, gather_cols, gather_p):
        g.finish()
    for n in range(8):
        p, b = order[n]
        to_sibling(n, ortho.at[b * 4 + p, core], bs_send, bs_recv).wait_send()
        cols_to_sibling(n).wait_send()
        poly_to_sibling(n).wait_send()
        for c in half_hops(n, p, b) + whole_hops(n, p, b):
            c.wait_send()
    for m in range(4):
        pair_hop(m, order[twos[m][0]][0]).wait_send()


def iterate(blended):
    dma = pltpu.SemaphoreType.DMA
    return pl.pallas_call(
        kernel,
        out_shape=jax.ShapeDtypeStruct((TILE, WIDTH), BF16),
        in_specs=[pl.BlockSpec(memory_space=pltpu.VMEM)],
        out_specs=pl.BlockSpec(memory_space=pltpu.VMEM),
        scratch_shapes=[
            pltpu.VMEM((8, TILE, WIDTH), BF16),
            pltpu.VMEM((8, 2, TILE, WIDTH), BF16),
            pltpu.VMEM((2, 4, TILE, BLOCK), F32),
            pltpu.VMEM((8, 2, 40, BLOCK), F32),
            pltpu.VMEM((8, 2, PIECE, BLOCK), F32),
            pltpu.VMEM((4, PIECE, BLOCK), F32),
            pltpu.VMEM((2, 4, 2, 4, PIECE, BLOCK), BF16),
            pltpu.VMEM((8, TILE, BLOCK), BF16),
            pltpu.VMEM((8, 2, TILE, BLOCK), BF16),
            pltpu.VMEM((TILE, BLOCK), F32),
            pltpu.VMEM((384, WIDTH), F32),
            pltpu.VMEM((4, 4, 8, 128), F32),
            dma((9,)), dma((9,)), dma((8,)), dma((8,)),
            dma((8, 2)), dma((8, 2)), dma((8, 2)), dma((8, 2)), dma((4,)), dma((4,)),
            dma((9,)), dma((9,)), dma((9,)), dma((9,)), dma((8,)), dma((8,)),
            dma((9,)), dma((9,)), dma((8,)), dma((8,)),
            dma((4, 3)), dma((4, 3)),
        ],
        compiler_params=pltpu.CompilerParams(
            collective_id=0, has_side_effects=True, vmem_limit_bytes=60 << 20
        ),
    )(blended)


def per_device(grad, momentum):
    new_momentum = momentum_decay * momentum + grad
    blended = (grad + momentum_decay * new_momentum).astype(BF16)
    return (iterate(blended), new_momentum)


def solution(mesh):
    placed = (P("row", "col"), P("row", "col"))
    return jax.shard_map(
        per_device,
        mesh=mesh,
        in_specs=placed,
        out_specs=(P("row", "col"), P("row", "col")),
        check_vma=False,
    )
```

```python
import math

import jax
import jax.numpy as jnp
from jax import lax
from jax.experimental import pallas as pl
from jax.experimental.pallas import tpu as pltpu
from jax.sharding import PartitionSpec as P

momentum_decay = 0.95
target_rms = 0.25
norm_epsilon = 1e-07
coef_linear = 3.4445
coef_cubic = -4.775
coef_quintic = 2.0315

MESH = pl.DeviceIdType.MESH
F32 = jnp.float32
BF16 = jnp.bfloat16

TILE = 320
BLOCK = 640
WIDTH = 1024
PIECE = 80


class Gather:
    def __init__(self, own, whole, some, rows, cut, p, b, right, left, pair, send, recv, across=0, cut_pair=None):
        def copy(n, src, dst, device):
            return pltpu.make_async_remote_copy(
                src, dst, send.at[n], recv.at[n], device_id=device, device_id_type=MESH
            )

        def on(n, p, b, first, size, device):
            place = some(p, b, first, size)
            return copy(n, place, place, device)

        lo, hi = lax.rem(p + 3, 4), lax.rem(p + 1, 4)
        opp = lax.rem(p + 2, 4)
        c = 1 - b
        own_place = whole(p, b)
        around = rows - across
        cut_pair = cut if cut_pair is None else cut_pair
        self.pair = copy(0, own, own_place, pair)
        self.right = copy(1, own, own_place, right)
        self.left = copy(2, own, own_place, left)
        self.right_pair = on(3, p, c, 0, around, right)
        self.left_pair = on(4, p, c, 0, around, left)
        self.on_right = on(5, lo, b, 0, cut, right)
        self.on_left = on(6, hi, b, cut, rows - cut, left)
        self.on_right_pair = on(7, lo, c, 0, cut_pair, right)
        self.on_left_pair = on(8, hi, c, cut_pair, around - cut_pair, left)
        self.all = [
            self.pair, self.right, self.left, self.right_pair, self.left_pair,
            self.on_right, self.on_left, self.on_right_pair, self.on_left_pair,
        ]
        self.across = []
        if across:
            self.across = [on(9 + k, q, b, around, across, pair) for k, q in enumerate((lo, hi, opp))]
            self.all = self.all + self.across
        self.order = [(p, b), (p, c), (lo, b), (hi, b), (lo, c), (hi, c), (opp, b), (opp, c)]

    def start(self):
        self.pair.start()
        self.right.start()
        self.left.start()

    def arrive(self, n):
        waits = {
            1: [self.pair], 2: [self.right], 3: [self.left], 4: [self.right_pair], 5: [self.left_pair],
            6: [self.on_right, self.on_left], 7: [self.on_right_pair, self.on_left_pair],
        }
        starts = {
            1: [self.right_pair, self.left_pair], 2: [self.on_right], 3: [self.on_left],
            4: [self.on_right_pair], 5: [self.on_left_pair],
        }
        if self.across:
            for block, k in ((2, 0), (3, 1), (6, 2)):
                starts[block] = starts.get(block, []) + [self.across[k]]
        for c in waits[n]:
            c.wait_recv()
        for c in starts.get(n, []):
            c.start()

    def arrive_across(self, n):
        if self.across:
            self.across[{4: 0, 5: 1, 7: 2}[n]].wait_recv()

    def finish(self):
        for c in self.all:
            c.wait_send()


def kernel(
    blended, out,
    raw, ortho, part, hop_half, hop_whole, hop_plane, hop_pair, gram_cols, gram_rows, poly, square, total, sums,
    b_send, b_recv, bs_send, bs_recv, half_send, half_recv, whole_send, whole_recv, plane_send, plane_recv, z_send, z_recv,
    gr_send, gr_recv, gc_send, gc_recv, gs_send, gs_recv, p_send, p_recv, ps_send, ps_recv,
    sum_send, sum_recv,
):
    row, col = lax.axis_index("row"), lax.axis_index("col")
    core = lax.rem(row, 2)
    x = lax.rem(lax.div(row, 2), 4)
    z_lo = lax.div(row, 8)
    y, z_hi = lax.div(col, 2), lax.rem(col, 2)
    chip_row = lax.div(row, 2)

    def at(x=x, y=y, z_lo=z_lo, z_hi=z_hi, core=core):
        return ((z_lo * 4 + x) * 2 + core, y * 2 + z_hi)

    def turn(v, n):
        return lax.rem(v + n, 4)

    sibling = at(core=1 - core)
    x_right, x_left = at(x=turn(x, 1)), at(x=turn(x, 3))
    y_right, y_left = at(y=turn(y, 1)), at(y=turn(y, 3))
    lo_pair, hi_pair = at(z_lo=1 - z_lo), at(z_hi=1 - z_hi)
    z = z_hi * 2 + z_lo
    peers = {
        "core": [sibling],
        "x": [at(x=turn(x, n)) for n in (1, 2, 3)],
        "y": [at(y=turn(y, n)) for n in (1, 2, 3)],
        "z": [at(z_lo=lax.rem(turn(z, n), 2), z_hi=lax.div(turn(z, n), 2)) for n in (1, 2, 3)],
    }
    everyone = [d for group in peers.values() for d in group]

    barrier = pltpu.get_barrier_semaphore()
    for d in everyone:
        pl.semaphore_signal(barrier, inc=1, device_id=d, device_id_type=MESH)
    pl.semaphore_wait(barrier, len(everyone))

    gather_b = Gather(
        blended,
        lambda p, b: raw.at[b * 4 + p],
        lambda p, b, first, rows: raw.at[b * 4 + p, pl.ds(first, rows)],
        TILE, 160, x, z_lo, x_right, x_left, lo_pair, b_send, b_recv,
    )
    gather_b.start()

    mine = jnp.zeros((8, 128), F32)
    for k in range(8):
        wide = blended[:, k * 128 : (k + 1) * 128].astype(F32).reshape(TILE // 8, 8, 128)
        mine = mine + jnp.sum(wide * wide, axis=0)
    for stage, (place, size) in enumerate(((core, 2), (x, 4), (y, 4), (z, 4))):
        group = list(peers.values())[stage]
        sums[stage, place] = mine
        copies = [
            pltpu.make_async_remote_copy(
                sums.at[stage, place], sums.at[stage, place],
                sum_send.at[stage, n], sum_recv.at[stage, n], device_id=d, device_id_type=MESH,
            )
            for n, d in enumerate(group)
        ]
        for c in copies:
            c.start()
        for c in copies:
            c.wait()
        mine = sums[stage, 0]
        for n in range(1, size):
            mine = mine + sums[stage, n]
    squares_total = jnp.sum(mine, keepdims=True)
    norm_scale = target_rms * math.sqrt(5120) / (jnp.sqrt(squares_total) + norm_epsilon)

    def to_sibling(n, src, send, recv):
        return pltpu.make_async_remote_copy(
            src, src, send.at[n], recv.at[n], device_id=sibling, device_id_type=MESH
        )

    mine_rows = pl.ds(pl.multiple_of(y * PIECE, PIECE), PIECE)

    def scale(src, j):
        def body(k, carry):
            rows = pl.ds(pl.multiple_of(k * 32, 32), 32)
            ortho[j, core, rows] = (src[rows].astype(F32) * norm_scale).astype(BF16)
            return carry

        lax.fori_loop(0, TILE // 32, body, 0)

    def partial(p, b):
        part[b, p] = lax.dot_general(
            ortho[b * 4 + p, core],
            ortho[chip_row].reshape(BLOCK, WIDTH),
            (((1,), (1,)), ((), ())),
            preferred_element_type=F32,
        )

    def half_hops(n, p, b):
        far = turn(y, 2) * PIECE
        return [
            pltpu.make_async_remote_copy(
                part.at[b, p, pl.ds(pl.multiple_of(far + 40 * k, 8), 40)],
                hop_half.at[n, k],
                half_send.at[n, k], half_recv.at[n, k], device_id=d, device_id_type=MESH,
            )
            for k, d in enumerate((y_right, y_left))
        ]

    def whole_hops(n, p, b):
        return [
            pltpu.make_async_remote_copy(
                part.at[b, p, pl.ds(pl.multiple_of(near * PIECE, 8), PIECE)],
                hop_whole.at[n, k],
                whole_send.at[n, k], whole_recv.at[n, k], device_id=d, device_id_type=MESH,
            )
            for k, (near, d) in enumerate(((turn(y, 1), y_right), (turn(y, 3), y_left)))
        ]

    order = gather_b.order
    lo, hi, opp = turn(x, 3), turn(x, 1), turn(x, 2)
    places = (x, lo, hi, opp)

    def plane_hop(m):
        return pltpu.make_async_remote_copy(
            part.at[1 - z_hi, places[m]], hop_plane.at[m],
            plane_send.at[m], plane_recv.at[m], device_id=hi_pair, device_id_type=MESH,
        )

    def pair_hop(m):
        return pltpu.make_async_remote_copy(
            part.at[1 - z_hi, places[m], mine_rows], hop_pair.at[m - 2],
            z_send.at[m - 2], z_recv.at[m - 2], device_id=hi_pair, device_id_type=MESH,
        )

    tasks = ((x, z_hi), (lo, z_hi), (hi, z_lo), (hi, 1 - z_lo), (opp, z_lo), (opp, 1 - z_lo))

    def reduce_1(t):
        for c in half_hops(t, *tasks[t]):
            c.start()

    def reduce_2(t):
        p, b = tasks[t]
        halves, wholes = half_hops(t, p, b), whole_hops(t, p, b)
        for k, near in enumerate((turn(y, 1), turn(y, 3))):
            halves[k].wait_recv()
            rows = pl.ds(pl.multiple_of(near * PIECE + 40 * k, 8), 40)
            part[b, p, rows] = part[b, p, rows] + hop_half[t, k]
            wholes[k].start()

    def reduce_3(t):
        p, b = tasks[t]
        for c in whole_hops(t, p, b):
            c.wait_recv()
        part[b, p, mine_rows] = part[b, p, mine_rows] + (hop_whole[t, 0] + hop_whole[t, 1])

    def add_planes(m):
        plane_hop(m).wait_recv()
        part[z_hi, places[m]] = part[z_hi, places[m]] + hop_plane[m]
        reduce_1(m)

    def finish_tile(m):
        p = places[m]
        tile = part[z_hi, p, mine_rows]
        if m >= 2:
            pair_hop(m).wait_recv()
            tile = tile + hop_pair[m - 2]
        tile = tile.astype(BF16)
        gram_cols[z_hi, p, core, y] = tile
        gram_rows[chip_row, pl.ds(pl.multiple_of(p * PIECE, 16), PIECE)] = tile

    def from_sibling(n):
        p, b = order[n]
        return to_sibling(n, ortho.at[b * 4 + p, core], bs_send, bs_recv)

    def process(n):
        p, b = order[n]
        scale(blended if n == 0 else raw.at[b * 4 + p], b * 4 + p)
        from_sibling(n).start()
        if n == 0:
            from_sibling(0).wait_recv()
        partial(p, b)

    def gather_rows(m):
        def place(p, b, first, rows):
            part_of = turn(p, (0, 3, 1, 2)[m]) * PIECE
            return gram_rows.at[b * 4 + p, pl.ds(pl.multiple_of(part_of + first, 16), rows)]

        return Gather(
            place(x, z_lo, 0, PIECE), lambda p, b: place(p, b, 0, PIECE), place,
            PIECE, 48, x, z_lo, x_right, x_left, lo_pair, gr_send.at[m], gr_recv.at[m],
        )

    def gather_cols(m):
        q = turn(x, (0, 3, 1, 2)[m])

        def place(p, b, first, rows):
            return gram_cols.at[b, q, core, p, pl.ds(first, rows)]

        return Gather(
            place(y, z_hi, 0, PIECE), lambda p, b: place(p, b, 0, PIECE), place,
            PIECE, 48, y, z_hi, y_right, y_left, hi_pair, gc_send.at[m], gc_recv.at[m],
        )

    def cols_to_sibling(m, n):
        p, b = cols_gathers[m].order[n]
        place = gram_cols.at[b, turn(x, (0, 3, 1, 2)[m]), core, p]
        return to_sibling(n, place, gs_send.at[m], gs_recv.at[m])

    rows_gathers = [gather_rows(m) for m in range(4)]
    cols_gathers = [gather_cols(m) for m in range(4)]

    def spread(m, event):
        if event == 0:
            finish_tile(m)
            cols_gathers[m].start()
            rows_gathers[m].start()
            cols_to_sibling(m, 0).start()
        for n in ((), (1, 2, 3), (4, 5), (6, 7))[event]:
            cols_gathers[m].arrive(n)
            cols_to_sibling(m, n).start()
            rows_gathers[m].arrive(n)

    process(0)
    for n in (1, 2, 3):
        gather_b.arrive(n)
    process(1)
    plane_hop(0).start()
    process(3)
    reduce_1(2)
    process(2)
    reduce_2(2)
    gather_b.arrive(4)
    gather_b.arrive(5)
    process(4)
    plane_hop(1).start()
    process(5)
    reduce_1(3)
    reduce_3(2)
    add_planes(0)
    reduce_2(3)
    gather_b.arrive(6)
    process(6)
    reduce_1(4)
    reduce_2(0)
    reduce_3(3)
    pair_hop(2).start()
    gather_b.arrive(7)
    process(7)
    reduce_1(5)
    reduce_2(4)
    reduce_3(0)
    spread(0, 0)
    reduce_2(5)
    spread(2, 0)
    add_planes(1)
    reduce_3(4)
    spread(0, 1)
    reduce_3(5)
    pair_hop(3).start()
    spread(2, 1)
    reduce_2(1)
    spread(0, 2)
    spread(2, 2)
    spread(3, 0)
    reduce_3(1)
    spread(1, 0)
    spread(0, 3)
    spread(2, 3)
    spread(3, 1)
    spread(1, 1)
    spread(3, 2)
    spread(1, 2)
    spread(3, 3)
    spread(1, 3)
    for m in range(4):
        for n in range(8):
            cols_to_sibling(m, n).wait_recv()

    def half_of_poly(h):
        rows = pl.ds(h * 160, 160)
        square[...] = jnp.zeros_like(square)

        def add_square(k, carry):
            right = gram_cols[lax.div(k, 4), lax.rem(k, 4)].reshape(BLOCK, BLOCK)
            square[...] += jnp.dot(gram_rows[k, rows], right, preferred_element_type=F32)
            return carry

        lax.fori_loop(0, 8, add_square, 0)
        poly[col, h, core] = (
            coef_cubic * gram_rows[chip_row, rows].astype(F32) + coef_quintic * square[...]
        ).astype(BF16)

    gathers_p = [
        Gather(
            poly.at[col, h, core],
            lambda p, b, h=h: poly.at[p * 2 + b, h, core],
            lambda p, b, first, rows, h=h: poly.at[p * 2 + b, h, core, pl.ds(first, rows)],
            160, 80, y, z_hi, y_right, y_left, hi_pair, p_send.at[h], p_recv.at[h], across=64, cut_pair=48,
        )
        for h in range(2)
    ]

    def poly_to_sibling(h, n):
        p, b = gathers_p[h].order[n]
        return to_sibling(n, poly.at[p * 2 + b, h, core], ps_send.at[h], ps_recv.at[h])

    for h in range(2):
        half_of_poly(h)
        gathers_p[h].start()
        poly_to_sibling(h, 0).start()

    for n in range(1, 8):
        from_sibling(n).wait_recv()

    lanes = pl.ds(pl.multiple_of(core * 256, 128), 384)
    total[...] = jnp.zeros_like(total)

    def add_product(h, n):
        poly_to_sibling(h, n).wait_recv()
        p, b = gathers_p[h].order[n]
        first = pl.multiple_of(p * PIECE, 16)
        left = poly[p * 2 + b, h, :, :, lanes].reshape(TILE, 384)
        right = jnp.concatenate(
            [ortho[b * 4 + 2 * h + k, a, pl.ds(first, PIECE)] for a in range(2) for k in range(2)], axis=0
        )
        total[...] += lax.dot_general(
            left, right, (((0,), (0,)), ((), ())), preferred_element_type=F32
        )

    for h in range(2):
        for n in (1, 2, 3):
            gathers_p[h].arrive(n)
            poly_to_sibling(h, n).start()
    for h in range(2):
        for n in range(4):
            add_product(h, n)
    for h in range(2):
        gathers_p[h].arrive(6)
        poly_to_sibling(h, 6).start()
        for n in (4, 5):
            gathers_p[h].arrive(n)
        for n in (4, 5):
            gathers_p[h].arrive_across(n)
            poly_to_sibling(h, n).start()
        for n in (4, 5, 6):
            add_product(h, n)
    for h in range(2):
        gathers_p[h].arrive(7)
        gathers_p[h].arrive_across(7)
        poly_to_sibling(h, 7).start()
    for h in range(2):
        add_product(h, 7)

    product = total[pl.ds(pl.multiple_of(core * 64, 8), TILE)]
    out[...] = (
        math.sqrt(8192) * (coef_linear * ortho[chip_row, core].astype(F32) + product)
    ).astype(BF16)

    gather_b.finish()
    for h in range(2):
        gathers_p[h].finish()
        for n in range(8):
            poly_to_sibling(h, n).wait_send()
    for n in range(8):
        from_sibling(n).wait_send()
    for t in range(6):
        for c in half_hops(t, *tasks[t]) + whole_hops(t, *tasks[t]):
            c.wait_send()
    for m in range(2):
        plane_hop(m).wait_send()
        pair_hop(m + 2).wait_send()
    for m in range(4):
        rows_gathers[m].finish()
        cols_gathers[m].finish()
        for n in range(8):
            cols_to_sibling(m, n).wait_send()


def iterate(blended):
    dma = pltpu.SemaphoreType.DMA
    return pl.pallas_call(
        kernel,
        out_shape=jax.ShapeDtypeStruct((TILE, WIDTH), BF16),
        in_specs=[pl.BlockSpec(memory_space=pltpu.VMEM)],
        out_specs=pl.BlockSpec(memory_space=pltpu.VMEM),
        scratch_shapes=[
            pltpu.VMEM((8, TILE, WIDTH), BF16),
            pltpu.VMEM((8, 2, TILE, WIDTH), BF16),
            pltpu.VMEM((2, 4, TILE, BLOCK), F32),
            pltpu.VMEM((6, 2, 40, BLOCK), F32),
            pltpu.VMEM((6, 2, PIECE, BLOCK), F32),
            pltpu.VMEM((2, TILE, BLOCK), F32),
            pltpu.VMEM((2, PIECE, BLOCK), F32),
            pltpu.VMEM((2, 4, 2, 4, PIECE, BLOCK), BF16),
            pltpu.VMEM((8, TILE, BLOCK), BF16),
            pltpu.VMEM((8, 2, 2, 160, BLOCK), BF16),
            pltpu.VMEM((160, BLOCK), F32),
            pltpu.VMEM((384, WIDTH), F32),
            pltpu.VMEM((4, 4, 8, 128), F32),
            dma((9,)), dma((9,)), dma((8,)), dma((8,)),
            dma((6, 2)), dma((6, 2)), dma((6, 2)), dma((6, 2)), dma((2,)), dma((2,)), dma((2,)), dma((2,)),
            dma((4, 9)), dma((4, 9)), dma((4, 9)), dma((4, 9)), dma((4, 8)), dma((4, 8)),
            dma((2, 12)), dma((2, 12)), dma((2, 8)), dma((2, 8)),
            dma((4, 3)), dma((4, 3)),
        ],
        compiler_params=pltpu.CompilerParams(
            collective_id=0, has_side_effects=True, vmem_limit_bytes=60 << 20
        ),
    )(blended)


def per_device(grad, momentum):
    new_momentum = momentum_decay * momentum + grad
    blended = (grad + momentum_decay * new_momentum).astype(BF16)
    return (iterate(blended), new_momentum)


def solution(mesh):
    placed = (P("row", "col"), P("row", "col"))
    return jax.shard_map(
        per_device,
        mesh=mesh,
        in_specs=placed,
        out_specs=(P("row", "col"), P("row", "col")),
        check_vma=False,
    )
```

```python
import math

import jax
import jax.numpy as jnp
from jax import lax
from jax.experimental import pallas as pl
from jax.experimental.pallas import tpu as pltpu
from jax.sharding import PartitionSpec as P

momentum_decay = 0.95
target_rms = 0.25
norm_epsilon = 1e-07
coef_linear = 3.4445
coef_cubic = -4.775
coef_quintic = 2.0315

MESH = pl.DeviceIdType.MESH
F32 = jnp.float32
BF16 = jnp.bfloat16

TILE = 320
BLOCK = 640
WIDTH = 1024
PIECE = 80


class Gather:
    def __init__(self, own, whole, some, rows, cut, p, b, right, left, pair, send, recv, across=0, cut_pair=None):
        def copy(n, src, dst, device):
            return pltpu.make_async_remote_copy(
                src, dst, send.at[n], recv.at[n], device_id=device, device_id_type=MESH
            )

        def on(n, p, b, first, size, device):
            place = some(p, b, first, size)
            return copy(n, place, place, device)

        lo, hi = lax.rem(p + 3, 4), lax.rem(p + 1, 4)
        opp = lax.rem(p + 2, 4)
        c = 1 - b
        own_place = whole(p, b)
        around = rows - across
        cut_pair = cut if cut_pair is None else cut_pair
        self.pair = copy(0, own, own_place, pair)
        self.right = copy(1, own, own_place, right)
        self.left = copy(2, own, own_place, left)
        self.right_pair = on(3, p, c, 0, around, right)
        self.left_pair = on(4, p, c, 0, around, left)
        self.on_right = on(5, lo, b, 0, cut, right)
        self.on_left = on(6, hi, b, cut, rows - cut, left)
        self.on_right_pair = on(7, lo, c, 0, cut_pair, right)
        self.on_left_pair = on(8, hi, c, cut_pair, around - cut_pair, left)
        self.all = [
            self.pair, self.right, self.left, self.right_pair, self.left_pair,
            self.on_right, self.on_left, self.on_right_pair, self.on_left_pair,
        ]
        self.across = []
        if across:
            self.across = [on(9 + k, q, b, around, across, pair) for k, q in enumerate((lo, hi, opp))]
            self.all = self.all + self.across
        self.order = [(p, b), (p, c), (lo, b), (hi, b), (lo, c), (hi, c), (opp, b), (opp, c)]

    def start(self):
        self.pair.start()
        self.right.start()
        self.left.start()

    def arrive(self, n):
        waits = {
            1: [self.pair], 2: [self.right], 3: [self.left], 4: [self.right_pair], 5: [self.left_pair],
            6: [self.on_right, self.on_left], 7: [self.on_right_pair, self.on_left_pair],
        }
        starts = {
            1: [self.right_pair, self.left_pair], 2: [self.on_right], 3: [self.on_left],
            4: [self.on_right_pair], 5: [self.on_left_pair],
        }
        if self.across:
            for block, k in ((2, 0), (3, 1), (6, 2)):
                starts[block] = starts.get(block, []) + [self.across[k]]
        for c in waits[n]:
            c.wait_recv()
        for c in starts.get(n, []):
            c.start()

    def arrive_across(self, n):
        if self.across:
            self.across[{4: 0, 5: 1, 7: 2}[n]].wait_recv()

    def finish(self):
        for c in self.all:
            c.wait_send()


def kernel(
    blended, out,
    raw, ortho, part, hop_half, hop_whole, hop_pair, turned, turned_in, spots, gram_cols, gram_rows, poly, square, total, sums,
    b_send, b_recv, l_send, l_recv, bs_send, bs_recv, half_send, half_recv, whole_send, whole_recv, t_send, t_recv, z_send, z_recv,
    gr_send, gr_recv, gc_send, gc_recv, gs_send, gs_recv, p_send, p_recv, ps_send, ps_recv,
    sum_send, sum_recv,
):
    row, col = lax.axis_index("row"), lax.axis_index("col")
    core = lax.rem(row, 2)
    x = lax.rem(lax.div(row, 2), 4)
    z_lo = lax.div(row, 8)
    y, z_hi = lax.div(col, 2), lax.rem(col, 2)
    chip_row = lax.div(row, 2)

    def at(x=x, y=y, z_lo=z_lo, z_hi=z_hi, core=core):
        return ((z_lo * 4 + x) * 2 + core, y * 2 + z_hi)

    def turn(v, n):
        return lax.rem(v + n, 4)

    sibling = at(core=1 - core)
    x_right, x_left = at(x=turn(x, 1)), at(x=turn(x, 3))
    y_right, y_left = at(y=turn(y, 1)), at(y=turn(y, 3))
    lo_pair, hi_pair = at(z_lo=1 - z_lo), at(z_hi=1 - z_hi)
    z = z_hi * 2 + z_lo
    peers = {
        "core": [sibling],
        "x": [at(x=turn(x, n)) for n in (1, 2, 3)],
        "z": [at(z_lo=lax.rem(turn(z, n), 2), z_hi=lax.div(turn(z, n), 2)) for n in (1, 2, 3)],
        "y": [at(y=turn(y, n)) for n in (1, 2, 3)],
    }
    everyone = [d for group in peers.values() for d in group]

    barrier = pltpu.get_barrier_semaphore()
    for d in everyone:
        pl.semaphore_signal(barrier, inc=1, device_id=d, device_id_type=MESH)
    pl.semaphore_wait(barrier, len(everyone))

    lo, hi, opp = turn(x, 3), turn(x, 1), turn(x, 2)
    high = lax.div(x, 2)
    to_opp = high * z_lo + (1 - high) * (1 - z_lo)
    from_opp = (1 - high) * z_lo + high * (1 - z_lo)

    def b_copy(n, b, device, first=0, rows=TILE):
        place = raw.at[b * 4 + x, pl.ds(first, rows)]
        return pltpu.make_async_remote_copy(
            place, place, b_send.at[n], b_recv.at[n], device_id=device, device_id_type=MESH
        )

    across = [b_copy(0, z_lo, lo_pair, 0, 128), b_copy(1, z_lo, lo_pair, 128, 192)]
    own_left = b_copy(2, z_lo, x_left)
    other_right = [b_copy(3, 1 - z_lo, x_right, 0, 128), b_copy(4, 1 - z_lo, x_right, 128, 192)]
    first_opp = b_copy(5, to_opp, at(x=opp))
    order = [
        (x, z_lo), (x, 1 - z_lo), (hi, z_lo), (lo, 1 - z_lo), (opp, from_opp),
        (hi, 1 - z_lo), (lo, z_lo), (opp, 1 - from_opp),
    ]
    raw[z_lo * 4 + x] = blended[...]
    across[0].start()

    mine = jnp.zeros((8, 128), F32)
    for k in range(8):
        wide = blended[:, k * 128 : (k + 1) * 128].astype(F32).reshape(TILE // 8, 8, 128)
        mine = mine + jnp.sum(wide * wide, axis=0)
    for stage, (place, size) in enumerate(((core, 2), (x, 4), (z, 4), (y, 4))):
        group = list(peers.values())[stage]
        sums[stage, place] = mine
        copies = [
            pltpu.make_async_remote_copy(
                sums.at[stage, place], sums.at[stage, place],
                sum_send.at[stage, n], sum_recv.at[stage, n], device_id=d, device_id_type=MESH,
            )
            for n, d in enumerate(group)
        ]
        for c in copies:
            c.start()
        for c in copies:
            c.wait()
        mine = sums[stage, 0]
        for n in range(1, size):
            mine = mine + sums[stage, n]
        if stage == 1:
            own_left.start()
            pl.when(high == 1)(first_opp.start)
        elif stage == 2:
            across[1].start()
    squares_total = jnp.sum(mine, keepdims=True)
    norm_scale = target_rms * math.sqrt(5120) / (jnp.sqrt(squares_total) + norm_epsilon)

    def to_sibling(n, src, send, recv):
        return pltpu.make_async_remote_copy(
            src, src, send.at[n], recv.at[n], device_id=sibling, device_id_type=MESH
        )

    mine_rows = pl.ds(pl.multiple_of(y * PIECE, PIECE), PIECE)

    def scale(src, j):
        def body(k, carry):
            rows = pl.ds(pl.multiple_of(k * 32, 32), 32)
            ortho[j, core, rows] = (src[rows].astype(F32) * norm_scale).astype(BF16)
            return carry

        lax.fori_loop(0, TILE // 32, body, 0)

    def partial(p, b):
        part[b, p] = lax.dot_general(
            ortho[b * 4 + p, core],
            ortho[chip_row].reshape(BLOCK, WIDTH),
            (((1,), (1,)), ((), ())),
            preferred_element_type=F32,
        )

    def half_hops(n, p, b):
        far = turn(y, 2) * PIECE
        return [
            pltpu.make_async_remote_copy(
                part.at[b, p, pl.ds(pl.multiple_of(far + 40 * k, 8), 40)],
                hop_half.at[n, k],
                half_send.at[n, k], half_recv.at[n, k], device_id=d, device_id_type=MESH,
            )
            for k, d in enumerate((y_right, y_left))
        ]

    def whole_hops(n, p, b):
        return [
            pltpu.make_async_remote_copy(
                part.at[b, p, pl.ds(pl.multiple_of(near * PIECE, 8), PIECE)],
                hop_whole.at[n, k],
                whole_send.at[n, k], whole_recv.at[n, k], device_id=d, device_id_type=MESH,
            )
            for k, (near, d) in enumerate(((turn(y, 1), y_right), (turn(y, 3), y_left)))
        ]

    places = (x, lo, hi, opp)

    planes = (None, 1 - z_lo, z_lo, from_opp)

    tasks = ((x, z_lo), (x, 1 - z_lo), (lo, 1 - z_lo), (hi, z_lo), (opp, from_opp))

    def reduce_1(t):
        partial(*tasks[t])
        for c in half_hops(t, *tasks[t]):
            c.start()

    def reduce_2(t):
        p, b = tasks[t]
        halves, wholes = half_hops(t, p, b), whole_hops(t, p, b)
        for k, near in enumerate((turn(y, 1), turn(y, 3))):
            halves[k].wait_recv()
            rows = pl.ds(pl.multiple_of(near * PIECE + 40 * k, 8), 40)
            part[b, p, rows] = part[b, p, rows] + hop_half[t, k]
            wholes[k].start()

    def reduce_3(t):
        p, b = tasks[t]
        for c in whole_hops(t, p, b):
            c.wait_recv()
        part[b, p, mine_rows] = part[b, p, mine_rows] + (hop_whole[t, 0] + hop_whole[t, 1])

    def pair_hop(m):
        b = 1 - z_hi if m == 0 else planes[m]
        return pltpu.make_async_remote_copy(
            part.at[b, places[m], mine_rows], hop_pair.at[m],
            z_send.at[m], z_recv.at[m], device_id=hi_pair, device_id_type=MESH,
        )

    def reduce_4(m):
        if m == 0:
            pair_hop(0).start()
        else:
            pl.when(planes[m] != z_hi)(lambda: pair_hop(m).start())

    def keep(m, tile):
        p = places[m]
        gram_cols[z_hi, p, core, y] = tile
        gram_rows[chip_row, pl.ds(pl.multiple_of(p * PIECE, 16), PIECE)] = tile

    def summed(m):
        pair_hop(m).wait_recv()
        return part[z_hi, places[m], mine_rows] + hop_pair[m]

    def turned_pieces(m):
        away = (0, 2, 1, 3)[m]
        return [
            pltpu.make_async_remote_copy(
                turned.at[m - 1, a * 4 + k], turned_in.at[away - 1, core * 4 + y],
                t_send.at[m - 1], t_recv.at[away - 1],
                device_id=((z_hi * 4 + places[m]) * 2 + a, k * 2 + z_lo), device_id_type=MESH,
            )
            for a in range(2) for k in range(4)
        ]

    def all_turned(m):
        return pltpu.make_async_remote_copy(
            turned.at[m - 1], turned_in.at[m - 1],
            t_send.at[m - 1], t_recv.at[m - 1], device_id=sibling, device_id_type=MESH,
        )

    def reduce_5(m):
        @pl.when(planes[m] == z_hi)
        def _():
            tile = summed(m)
            keep(m, tile.astype(BF16))
            tall = jnp.concatenate([tile, jnp.zeros((128 - PIECE, BLOCK), F32)], axis=0).T
            turned[m - 1] = tall.astype(BF16).reshape(8, PIECE, 128)
            for c in turned_pieces(m):
                c.start()

    def finish_tile(m):
        if m == 0:
            keep(0, summed(0).astype(BF16))
            return

        @pl.when(planes[m] != z_hi)
        def _():
            all_turned(m).wait_recv()
            wide = jnp.concatenate([turned_in[m - 1, k] for k in range(8)], axis=1)
            keep(m, jnp.dot(wide, spots[...], preferred_element_type=F32).astype(BF16))

    def from_sibling(n):
        p, b = order[n]
        return to_sibling(n, ortho.at[b * 4 + p, core], bs_send, bs_recv)

    def later(k):
        p, b = order[2 + k // 4]
        place = ortho.at[b * 4 + p, core, pl.ds(k % 4 * 80, 80)]
        return pltpu.make_async_remote_copy(
            place, place, l_send.at[k], l_recv.at[k], device_id=lo_pair, device_id_type=MESH
        )

    def process(n):
        p, b = order[n]
        scale(raw.at[b * 4 + p], b * 4 + p)
        from_sibling(n).start()
        if n == 0:
            from_sibling(0).wait_recv()

    def gather_rows(m):
        def place(p, b, first, rows):
            part_of = turn(p, (0, 3, 1, 2)[m]) * PIECE
            return gram_rows.at[b * 4 + p, pl.ds(pl.multiple_of(part_of + first, 16), rows)]

        return Gather(
            place(x, z_lo, 0, PIECE), lambda p, b: place(p, b, 0, PIECE), place,
            PIECE, 48, x, z_lo, x_right, x_left, lo_pair, gr_send.at[m], gr_recv.at[m],
        )

    def gather_cols(m):
        q = turn(x, (0, 3, 1, 2)[m])

        def place(p, b, first, rows):
            return gram_cols.at[b, q, core, p, pl.ds(first, rows)]

        return Gather(
            place(y, z_hi, 0, PIECE), lambda p, b: place(p, b, 0, PIECE), place,
            PIECE, 48, y, z_hi, y_right, y_left, hi_pair, gc_send.at[m], gc_recv.at[m],
        )

    def cols_to_sibling(m, n):
        p, b = cols_gathers[m].order[n]
        place = gram_cols.at[b, turn(x, (0, 3, 1, 2)[m]), core, p]
        return to_sibling(n, place, gs_send.at[m], gs_recv.at[m])

    rows_gathers = [gather_rows(m) for m in range(4)]
    cols_gathers = [gather_cols(m) for m in range(4)]

    def spread(m, event):
        if event == 0:
            finish_tile(m)
            cols_gathers[m].start()
            rows_gathers[m].start()
            cols_to_sibling(m, 0).start()
        for n in ((), (1, 2, 3), (4, 5), (6, 7))[event]:
            cols_gathers[m].arrive(n)
            cols_to_sibling(m, n).start()
            rows_gathers[m].arrive(n)

    spot = lax.broadcasted_iota(jnp.int32, (WIDTH, BLOCK), 0)
    column = lax.broadcasted_iota(jnp.int32, (WIDTH, BLOCK), 1)
    lane = spot % 128
    spots[...] = jnp.where((lane < PIECE) & (column == spot // 128 * PIECE + lane), 1.0, 0.0).astype(BF16)

    across[0].wait_recv()
    other_right[0].start()
    process(0)
    reduce_1(0)
    across[1].wait_recv()
    other_right[1].start()
    pl.when(high == 0)(first_opp.start)
    process(1)
    reduce_1(1)
    reduce_2(0)
    own_left.wait_recv()
    process(2)
    reduce_1(3)
    reduce_2(1)
    for k in range(4):
        later(k).start()
    reduce_3(0)
    reduce_2(3)
    reduce_3(1)
    reduce_4(0)
    for c in other_right:
        c.wait_recv()
    process(3)
    reduce_1(2)
    reduce_3(3)
    reduce_4(2)
    later(4).start()
    later(5).start()
    first_opp.wait_recv()
    process(4)
    reduce_1(4)
    spread(0, 0)
    reduce_2(2)
    reduce_5(2)
    reduce_2(4)
    later(6).start()
    spread(0, 1)
    later(7).start()
    reduce_3(2)
    reduce_4(1)
    reduce_3(4)
    reduce_4(3)
    spread(0, 2)
    reduce_5(1)
    spread(1, 0)
    reduce_5(3)
    later(8).start()
    spread(2, 0)
    spread(0, 3)
    spread(1, 1)
    later(9).start()
    spread(3, 0)
    spread(2, 1)
    spread(1, 2)
    later(10).start()
    spread(3, 1)
    later(11).start()
    spread(2, 2)
    spread(3, 2)
    spread(1, 3)
    spread(2, 3)
    spread(3, 3)
    for m in range(4):
        for n in range(8):
            cols_to_sibling(m, n).wait_recv()

    def half_of_poly(h):
        rows = pl.ds(h * 160, 160)
        square[...] = jnp.zeros_like(square)

        def add_square(k, carry):
            right = gram_cols[lax.div(k, 4), lax.rem(k, 4)].reshape(BLOCK, BLOCK)
            square[...] += jnp.dot(gram_rows[k, rows], right, preferred_element_type=F32)
            return carry

        lax.fori_loop(0, 8, add_square, 0)
        poly[col, h, core] = (
            coef_cubic * gram_rows[chip_row, rows].astype(F32) + coef_quintic * square[...]
        ).astype(BF16)

    gathers_p = [
        Gather(
            poly.at[col, h, core],
            lambda p, b, h=h: poly.at[p * 2 + b, h, core],
            lambda p, b, first, rows, h=h: poly.at[p * 2 + b, h, core, pl.ds(first, rows)],
            160, 80, y, z_hi, y_right, y_left, hi_pair, p_send.at[h], p_recv.at[h], across=64, cut_pair=48,
        )
        for h in range(2)
    ]

    def poly_to_sibling(h, n):
        p, b = gathers_p[h].order[n]
        return to_sibling(n, poly.at[p * 2 + b, h, core], ps_send.at[h], ps_recv.at[h])

    for h in range(2):
        half_of_poly(h)
        gathers_p[h].start()
        poly_to_sibling(h, 0).start()

    for k in range(12):
        later(k).wait_recv()
        if k % 4 == 3:
            from_sibling(5 + k // 4).start()
    for n in range(1, 8):
        from_sibling(n).wait_recv()

    lanes = pl.ds(pl.multiple_of(core * 256, 128), 384)
    total[...] = jnp.zeros_like(total)

    def add_product(h, n):
        poly_to_sibling(h, n).wait_recv()
        p, b = gathers_p[h].order[n]
        first = pl.multiple_of(p * PIECE, 16)
        left = poly[p * 2 + b, h, :, :, lanes].reshape(TILE, 384)
        right = jnp.concatenate(
            [ortho[b * 4 + 2 * h + k, a, pl.ds(first, PIECE)] for a in range(2) for k in range(2)], axis=0
        )
        total[...] += lax.dot_general(
            left, right, (((0,), (0,)), ((), ())), preferred_element_type=F32
        )

    for h in range(2):
        for n in (1, 2, 3):
            gathers_p[h].arrive(n)
            poly_to_sibling(h, n).start()
    for h in range(2):
        for n in range(4):
            add_product(h, n)
    for h in range(2):
        gathers_p[h].arrive(6)
        poly_to_sibling(h, 6).start()
        for n in (4, 5):
            gathers_p[h].arrive(n)
        for n in (4, 5):
            gathers_p[h].arrive_across(n)
            poly_to_sibling(h, n).start()
        for n in (4, 5, 6):
            add_product(h, n)
    for h in range(2):
        gathers_p[h].arrive(7)
        gathers_p[h].arrive_across(7)
        poly_to_sibling(h, 7).start()
    for h in range(2):
        add_product(h, 7)

    product = total[pl.ds(pl.multiple_of(core * 64, 8), TILE)]
    out[...] = (
        math.sqrt(8192) * (coef_linear * ortho[chip_row, core].astype(F32) + product)
    ).astype(BF16)

    for c in across + other_right + [own_left, first_opp] + [later(k) for k in range(12)]:
        c.wait_send()
    for h in range(2):
        gathers_p[h].finish()
        for n in range(8):
            poly_to_sibling(h, n).wait_send()
    for n in range(8):
        from_sibling(n).wait_send()
    for t in range(5):
        for c in half_hops(t, *tasks[t]) + whole_hops(t, *tasks[t]):
            c.wait_send()
    pair_hop(0).wait_send()
    for m in (1, 2, 3):
        pl.when(planes[m] != z_hi)(lambda m=m: pair_hop(m).wait_send())
        pl.when(planes[m] == z_hi)(lambda m=m: all_turned(m).wait_send())
    for m in range(4):
        rows_gathers[m].finish()
        cols_gathers[m].finish()
        for n in range(8):
            cols_to_sibling(m, n).wait_send()


def iterate(blended):
    dma = pltpu.SemaphoreType.DMA
    return pl.pallas_call(
        kernel,
        out_shape=jax.ShapeDtypeStruct((TILE, WIDTH), BF16),
        in_specs=[pl.BlockSpec(memory_space=pltpu.VMEM)],
        out_specs=pl.BlockSpec(memory_space=pltpu.VMEM),
        scratch_shapes=[
            pltpu.VMEM((8, TILE, WIDTH), BF16),
            pltpu.VMEM((8, 2, TILE, WIDTH), BF16),
            pltpu.VMEM((2, 4, TILE, BLOCK), F32),
            pltpu.VMEM((5, 2, 40, BLOCK), F32),
            pltpu.VMEM((5, 2, PIECE, BLOCK), F32),
            pltpu.VMEM((4, PIECE, BLOCK), F32),
            pltpu.VMEM((3, 8, PIECE, 128), BF16),
            pltpu.VMEM((3, 8, PIECE, 128), BF16),
            pltpu.VMEM((WIDTH, BLOCK), BF16),
            pltpu.VMEM((2, 4, 2, 4, PIECE, BLOCK), BF16),
            pltpu.VMEM((8, TILE, BLOCK), BF16),
            pltpu.VMEM((8, 2, 2, 160, BLOCK), BF16),
            pltpu.VMEM((160, BLOCK), F32),
            pltpu.VMEM((384, WIDTH), F32),
            pltpu.VMEM((4, 4, 8, 128), F32),
            dma((6,)), dma((6,)), dma((12,)), dma((12,)), dma((8,)), dma((8,)),
            dma((5, 2)), dma((5, 2)), dma((5, 2)), dma((5, 2)), dma((3,)), dma((3,)), dma((4,)), dma((4,)),
            dma((4, 9)), dma((4, 9)), dma((4, 9)), dma((4, 9)), dma((4, 8)), dma((4, 8)),
            dma((2, 12)), dma((2, 12)), dma((2, 8)), dma((2, 8)),
            dma((4, 3)), dma((4, 3)),
        ],
        compiler_params=pltpu.CompilerParams(
            collective_id=0, has_side_effects=True, vmem_limit_bytes=60 << 20
        ),
    )(blended)


def per_device(grad, momentum):
    new_momentum = momentum_decay * momentum + grad
    blended = (grad + momentum_decay * new_momentum).astype(BF16)
    return (iterate(blended), new_momentum)


def solution(mesh):
    placed = (P("row", "col"), P("row", "col"))
    return jax.shard_map(
        per_device,
        mesh=mesh,
        in_specs=placed,
        out_specs=(P("row", "col"), P("row", "col")),
        check_vma=False,
    )
```

```python
import math

import jax
import jax.numpy as jnp
from jax import lax
from jax.experimental import pallas as pl
from jax.experimental.pallas import tpu as pltpu
from jax.sharding import PartitionSpec as P

momentum_decay = 0.95
target_rms = 0.25
norm_epsilon = 1e-07
coef_linear = 3.4445
coef_cubic = -4.775
coef_quintic = 2.0315

MESH = pl.DeviceIdType.MESH
F32 = jnp.float32
BF16 = jnp.bfloat16

TILE = 320
BLOCK = 640
WIDTH = 1024
PIECE = 80


class Gather:
    def __init__(self, own, whole, some, rows, cut, p, b, right, left, pair, send, recv, across=0, cut_pair=None):
        def copy(n, src, dst, device):
            return pltpu.make_async_remote_copy(
                src, dst, send.at[n], recv.at[n], device_id=device, device_id_type=MESH
            )

        def on(n, p, b, first, size, device):
            place = some(p, b, first, size)
            return copy(n, place, place, device)

        lo, hi = lax.rem(p + 3, 4), lax.rem(p + 1, 4)
        opp = lax.rem(p + 2, 4)
        c = 1 - b
        own_place = whole(p, b)
        around = rows - across
        cut_pair = cut if cut_pair is None else cut_pair
        self.pair = copy(0, own, own_place, pair)
        self.right = copy(1, own, own_place, right)
        self.left = copy(2, own, own_place, left)
        self.right_pair = on(3, p, c, 0, around, right)
        self.left_pair = on(4, p, c, 0, around, left)
        self.on_right = on(5, lo, b, 0, cut, right)
        self.on_left = on(6, hi, b, cut, rows - cut, left)
        self.on_right_pair = on(7, lo, c, 0, cut_pair, right)
        self.on_left_pair = on(8, hi, c, cut_pair, around - cut_pair, left)
        self.all = [
            self.pair, self.right, self.left, self.right_pair, self.left_pair,
            self.on_right, self.on_left, self.on_right_pair, self.on_left_pair,
        ]
        self.across = []
        if across:
            self.across = [on(9 + k, q, b, around, across, pair) for k, q in enumerate((lo, hi, opp))]
            self.all = self.all + self.across
        self.order = [(p, b), (p, c), (lo, b), (hi, b), (lo, c), (hi, c), (opp, b), (opp, c)]

    def start(self):
        self.pair.start()
        self.right.start()
        self.left.start()

    def arrive(self, n):
        waits = {
            1: [self.pair], 2: [self.right], 3: [self.left], 4: [self.right_pair], 5: [self.left_pair],
            6: [self.on_right, self.on_left], 7: [self.on_right_pair, self.on_left_pair],
        }
        starts = {
            1: [self.right_pair, self.left_pair], 2: [self.on_right], 3: [self.on_left],
            4: [self.on_right_pair], 5: [self.on_left_pair],
        }
        if self.across:
            for block, k in ((2, 0), (3, 1), (6, 2)):
                starts[block] = starts.get(block, []) + [self.across[k]]
        for c in waits[n]:
            c.wait_recv()
        for c in starts.get(n, []):
            c.start()

    def arrive_across(self, n):
        if self.across:
            self.across[{4: 0, 5: 1, 7: 2}[n]].wait_recv()

    def finish(self):
        for c in self.all:
            c.wait_send()


def kernel(
    blended, out,
    raw, ortho, part, hop_half, hop_whole, hop_pair, turned, turned_in, spots, gram_cols, gram_rows, poly, square, total, sums,
    b_send, b_recv, l_send, l_recv, bs_send, bs_recv, half_send, half_recv, whole_send, whole_recv, t_send, t_recv, z_send, z_recv,
    gr_send, gr_recv, gc_send, gc_recv, gs_send, gs_recv, p_send, p_recv, ps_send, ps_recv,
    sum_send, sum_recv,
):
    row, col = lax.axis_index("row"), lax.axis_index("col")
    core = lax.rem(row, 2)
    x = lax.rem(lax.div(row, 2), 4)
    z_lo = lax.div(row, 8)
    y, z_hi = lax.div(col, 2), lax.rem(col, 2)
    chip_row = lax.div(row, 2)

    def at(x=x, y=y, z_lo=z_lo, z_hi=z_hi, core=core):
        return ((z_lo * 4 + x) * 2 + core, y * 2 + z_hi)

    def turn(v, n):
        return lax.rem(v + n, 4)

    sibling = at(core=1 - core)
    x_right, x_left = at(x=turn(x, 1)), at(x=turn(x, 3))
    y_right, y_left = at(y=turn(y, 1)), at(y=turn(y, 3))
    lo_pair, hi_pair = at(z_lo=1 - z_lo), at(z_hi=1 - z_hi)
    z = z_hi * 2 + z_lo
    peers = {
        "core": [sibling],
        "x": [at(x=turn(x, n)) for n in (1, 2, 3)],
        "z": [at(z_lo=lax.rem(turn(z, n), 2), z_hi=lax.div(turn(z, n), 2)) for n in (1, 2, 3)],
        "y": [at(y=turn(y, n)) for n in (1, 2, 3)],
    }
    everyone = [d for group in peers.values() for d in group]

    barrier = pltpu.get_barrier_semaphore()
    for d in everyone:
        pl.semaphore_signal(barrier, inc=1, device_id=d, device_id_type=MESH)
    pl.semaphore_wait(barrier, len(everyone))

    lo, hi, opp = turn(x, 3), turn(x, 1), turn(x, 2)
    high = lax.div(x, 2)
    to_opp = high * z_lo + (1 - high) * (1 - z_lo)
    from_opp = (1 - high) * z_lo + high * (1 - z_lo)

    def b_copy(n, b, device, first=0, rows=TILE):
        place = raw.at[b * 4 + x, pl.ds(first, rows)]
        return pltpu.make_async_remote_copy(
            place, place, b_send.at[n], b_recv.at[n], device_id=device, device_id_type=MESH
        )

    across = [b_copy(0, z_lo, lo_pair, 0, 128), b_copy(1, z_lo, lo_pair, 128, 192)]
    own_left = b_copy(2, z_lo, x_left)
    other_right = [b_copy(3, 1 - z_lo, x_right, 0, 128), b_copy(4, 1 - z_lo, x_right, 128, 192)]
    first_opp = b_copy(5, to_opp, at(x=opp))
    order = [
        (x, z_lo), (x, 1 - z_lo), (hi, z_lo), (lo, 1 - z_lo), (opp, from_opp),
        (hi, 1 - z_lo), (lo, z_lo), (opp, 1 - from_opp),
    ]
    raw[z_lo * 4 + x] = blended[...]
    across[0].start()

    mine = jnp.zeros((8, 128), F32)
    for k in range(8):
        wide = blended[:, k * 128 : (k + 1) * 128].astype(F32).reshape(TILE // 8, 8, 128)
        mine = mine + jnp.sum(wide * wide, axis=0)
    for stage, (place, size) in enumerate(((core, 2), (x, 4), (z, 4), (y, 4))):
        group = list(peers.values())[stage]
        sums[stage, place] = mine
        copies = [
            pltpu.make_async_remote_copy(
                sums.at[stage, place], sums.at[stage, place],
                sum_send.at[stage, n], sum_recv.at[stage, n], device_id=d, device_id_type=MESH,
            )
            for n, d in enumerate(group)
        ]
        for c in copies:
            c.start()
        for c in copies:
            c.wait()
        mine = sums[stage, 0]
        for n in range(1, size):
            mine = mine + sums[stage, n]
        if stage == 1:
            own_left.start()
            pl.when(high == 1)(first_opp.start)
        elif stage == 2:
            across[1].start()
    squares_total = jnp.sum(mine, keepdims=True)
    norm_scale = target_rms * math.sqrt(5120) / (jnp.sqrt(squares_total) + norm_epsilon)

    def to_sibling(n, src, send, recv):
        return pltpu.make_async_remote_copy(
            src, src, send.at[n], recv.at[n], device_id=sibling, device_id_type=MESH
        )

    mine_rows = pl.ds(pl.multiple_of(y * PIECE, PIECE), PIECE)

    def scale(src, j):
        def body(k, carry):
            rows = pl.ds(pl.multiple_of(k * 32, 32), 32)
            ortho[j, core, rows] = (src[rows].astype(F32) * norm_scale).astype(BF16)
            return carry

        lax.fori_loop(0, TILE // 32, body, 0)

    def partial(p, b):
        part[b, p] = lax.dot_general(
            ortho[b * 4 + p, core],
            ortho[chip_row].reshape(BLOCK, WIDTH),
            (((1,), (1,)), ((), ())),
            preferred_element_type=F32,
        )

    def half_hops(n, p, b):
        far = turn(y, 2) * PIECE
        return [
            pltpu.make_async_remote_copy(
                part.at[b, p, pl.ds(pl.multiple_of(far + 40 * k, 8), 40)],
                hop_half.at[n, k],
                half_send.at[n, k], half_recv.at[n, k], device_id=d, device_id_type=MESH,
            )
            for k, d in enumerate((y_right, y_left))
        ]

    def whole_hops(n, p, b):
        return [
            pltpu.make_async_remote_copy(
                part.at[b, p, pl.ds(pl.multiple_of(near * PIECE, 8), PIECE)],
                hop_whole.at[n, k],
                whole_send.at[n, k], whole_recv.at[n, k], device_id=d, device_id_type=MESH,
            )
            for k, (near, d) in enumerate(((turn(y, 1), y_right), (turn(y, 3), y_left)))
        ]

    places = (x, lo, hi, opp)

    planes = (None, 1 - z_lo, z_lo, from_opp)

    tasks = ((x, z_lo), (x, 1 - z_lo), (lo, 1 - z_lo), (hi, z_lo), (opp, from_opp))

    def reduce_1(t):
        partial(*tasks[t])
        for c in half_hops(t, *tasks[t]):
            c.start()

    def reduce_2(t):
        p, b = tasks[t]
        halves, wholes = half_hops(t, p, b), whole_hops(t, p, b)
        for k, near in enumerate((turn(y, 1), turn(y, 3))):
            halves[k].wait_recv()
            rows = pl.ds(pl.multiple_of(near * PIECE + 40 * k, 8), 40)
            part[b, p, rows] = part[b, p, rows] + hop_half[t, k]
            wholes[k].start()

    def reduce_3(t):
        p, b = tasks[t]
        for c in whole_hops(t, p, b):
            c.wait_recv()
        part[b, p, mine_rows] = part[b, p, mine_rows] + (hop_whole[t, 0] + hop_whole[t, 1])

    def pair_hop(m):
        b = 1 - z_hi if m == 0 else planes[m]
        return pltpu.make_async_remote_copy(
            part.at[b, places[m], mine_rows], hop_pair.at[m],
            z_send.at[m], z_recv.at[m], device_id=hi_pair, device_id_type=MESH,
        )

    def reduce_4(m):
        if m == 0:
            pair_hop(0).start()
        else:
            pl.when(planes[m] != z_hi)(lambda: pair_hop(m).start())

    def keep(m, tile):
        p = places[m]
        gram_cols[z_hi, p, core, y] = tile
        gram_rows[chip_row, pl.ds(pl.multiple_of(p * PIECE, 16), PIECE)] = tile

    def summed(m):
        pair_hop(m).wait_recv()
        return part[z_hi, places[m], mine_rows] + hop_pair[m]

    def turned_pieces(m):
        away = (0, 2, 1, 3)[m]
        return [
            pltpu.make_async_remote_copy(
                turned.at[m - 1, a * 4 + k], turned_in.at[away - 1, core * 4 + y],
                t_send.at[m - 1], t_recv.at[away - 1],
                device_id=((z_hi * 4 + places[m]) * 2 + a, k * 2 + z_lo), device_id_type=MESH,
            )
            for a in range(2) for k in range(4)
        ]

    def all_turned(m):
        return pltpu.make_async_remote_copy(
            turned.at[m - 1], turned_in.at[m - 1],
            t_send.at[m - 1], t_recv.at[m - 1], device_id=sibling, device_id_type=MESH,
        )

    def reduce_5(m):
        @pl.when(planes[m] == z_hi)
        def _():
            tile = summed(m)
            keep(m, tile.astype(BF16))
            tall = jnp.concatenate([tile, jnp.zeros((128 - PIECE, BLOCK), F32)], axis=0).T
            turned[m - 1] = tall.astype(BF16).reshape(8, PIECE, 128)
            for c in turned_pieces(m):
                c.start()

    def finish_tile(m):
        if m == 0:
            keep(0, summed(0).astype(BF16))
            return

        @pl.when(planes[m] != z_hi)
        def _():
            all_turned(m).wait_recv()
            wide = jnp.concatenate([turned_in[m - 1, k] for k in range(8)], axis=1)
            keep(m, jnp.dot(wide, spots[...], preferred_element_type=F32).astype(BF16))

    def from_sibling(n):
        p, b = order[n]
        return to_sibling(n, ortho.at[b * 4 + p, core], bs_send, bs_recv)

    def later(k):
        if k == 8:
            place = ortho.at[(1 - to_opp) * 4 + x, core]
            return pltpu.make_async_remote_copy(
                place, place, l_send.at[8], l_recv.at[8], device_id=at(x=opp), device_id_type=MESH
            )
        p, b = order[2 + k // 4]
        place = ortho.at[b * 4 + p, core, pl.ds(k % 4 * 80, 80)]
        return pltpu.make_async_remote_copy(
            place, place, l_send.at[k], l_recv.at[k], device_id=lo_pair, device_id_type=MESH
        )

    def process(n):
        p, b = order[n]
        scale(raw.at[b * 4 + p], b * 4 + p)
        from_sibling(n).start()
        if n == 0:
            from_sibling(0).wait_recv()

    def gather_rows(m):
        def place(p, b, first, rows):
            part_of = turn(p, (0, 3, 1, 2)[m]) * PIECE
            return gram_rows.at[b * 4 + p, pl.ds(pl.multiple_of(part_of + first, 16), rows)]

        return Gather(
            place(x, z_lo, 0, PIECE), lambda p, b: place(p, b, 0, PIECE), place,
            PIECE, 48, x, z_lo, x_right, x_left, lo_pair, gr_send.at[m], gr_recv.at[m],
        )

    def gather_cols(m):
        q = turn(x, (0, 3, 1, 2)[m])

        def place(p, b, first, rows):
            return gram_cols.at[b, q, core, p, pl.ds(first, rows)]

        return Gather(
            place(y, z_hi, 0, PIECE), lambda p, b: place(p, b, 0, PIECE), place,
            PIECE, 48, y, z_hi, y_right, y_left, hi_pair, gc_send.at[m], gc_recv.at[m],
        )

    def cols_to_sibling(m, n):
        p, b = cols_gathers[m].order[n]
        place = gram_cols.at[b, turn(x, (0, 3, 1, 2)[m]), core, p]
        return to_sibling(n, place, gs_send.at[m], gs_recv.at[m])

    rows_gathers = [gather_rows(m) for m in range(4)]
    cols_gathers = [gather_cols(m) for m in range(4)]

    def spread(m, event):
        if event == 0:
            finish_tile(m)
            cols_gathers[m].start()
            rows_gathers[m].start()
            cols_to_sibling(m, 0).start()
        for n in ((), (1, 2, 3), (4, 5), (6, 7))[event]:
            cols_gathers[m].arrive(n)
            cols_to_sibling(m, n).start()
            rows_gathers[m].arrive(n)

    spot = lax.broadcasted_iota(jnp.int32, (WIDTH, BLOCK), 0)
    column = lax.broadcasted_iota(jnp.int32, (WIDTH, BLOCK), 1)
    lane = spot % 128
    spots[...] = jnp.where((lane < PIECE) & (column == spot // 128 * PIECE + lane), 1.0, 0.0).astype(BF16)

    across[0].wait_recv()
    other_right[0].start()
    process(0)
    reduce_1(0)
    across[1].wait_recv()
    other_right[1].start()
    pl.when(high == 0)(first_opp.start)
    process(1)
    reduce_1(1)
    reduce_2(0)
    own_left.wait_recv()
    process(2)
    reduce_1(3)
    reduce_2(1)
    for k in range(4):
        later(k).start()
    reduce_3(0)
    reduce_2(3)
    reduce_3(1)
    reduce_4(0)
    for c in other_right:
        c.wait_recv()
    process(3)
    reduce_1(2)
    reduce_3(3)
    reduce_4(2)
    later(4).start()
    later(5).start()
    first_opp.wait_recv()
    process(4)
    reduce_1(4)
    spread(0, 0)
    reduce_2(2)
    reduce_5(2)
    reduce_2(4)
    later(6).start()
    spread(0, 1)
    later(7).start()
    reduce_3(2)
    reduce_4(1)
    reduce_3(4)
    reduce_4(3)
    spread(0, 2)
    reduce_5(1)
    spread(1, 0)
    reduce_5(3)
    spread(2, 0)
    spread(0, 3)
    spread(1, 1)
    spread(3, 0)
    spread(2, 1)
    spread(1, 2)
    spread(3, 1)
    spread(2, 2)
    spread(3, 2)
    spread(1, 3)
    spread(2, 3)
    spread(3, 3)
    for m in range(4):
        for n in range(8):
            cols_to_sibling(m, n).wait_recv()

    def half_of_poly(h):
        rows = pl.ds(h * 160, 160)
        square[...] = jnp.zeros_like(square)

        def add_square(k, carry):
            right = gram_cols[lax.div(k, 4), lax.rem(k, 4)].reshape(BLOCK, BLOCK)
            square[...] += jnp.dot(gram_rows[k, rows], right, preferred_element_type=F32)
            return carry

        lax.fori_loop(0, 8, add_square, 0)
        poly[col, h, core] = (
            coef_cubic * gram_rows[chip_row, rows].astype(F32) + coef_quintic * square[...]
        ).astype(BF16)

    gathers_p = [
        Gather(
            poly.at[col, h, core],
            lambda p, b, h=h: poly.at[p * 2 + b, h, core],
            lambda p, b, first, rows, h=h: poly.at[p * 2 + b, h, core, pl.ds(first, rows)],
            160, 80, y, z_hi, y_right, y_left, hi_pair, p_send.at[h], p_recv.at[h], across=64, cut_pair=48,
        )
        for h in range(2)
    ]

    def poly_to_sibling(h, n):
        p, b = gathers_p[h].order[n]
        return to_sibling(n, poly.at[p * 2 + b, h, core], ps_send.at[h], ps_recv.at[h])

    later(8).start()
    for h in range(2):
        half_of_poly(h)
        gathers_p[h].start()
        poly_to_sibling(h, 0).start()

    lanes = pl.ds(pl.multiple_of(core * 256, 128), 384)
    total[...] = jnp.zeros_like(total)

    def add_product(n, columns):
        p, b = gathers_p[0].order[n]
        first = pl.multiple_of(p * PIECE, 16)
        left = [
            poly[p * 2 + b, lax.div(q, 2), a, pl.ds(pl.multiple_of(lax.rem(q, 2) * PIECE, 16), PIECE), lanes]
            for q in columns for a in range(2)
        ]
        right = [ortho[b * 4 + q, a, pl.ds(first, PIECE)] for q in columns for a in range(2)]
        total[...] += lax.dot_general(
            jnp.concatenate(left, axis=0), jnp.concatenate(right, axis=0),
            (((0,), (0,)), ((), ())), preferred_element_type=F32,
        )

    near, far = (x, hi), (lo, opp)

    for h in range(2):
        for n in (1, 2, 3):
            gathers_p[h].arrive(n)
            poly_to_sibling(h, n).start()
    for k in range(8):
        later(k).wait_recv()
        if k % 4 == 3:
            from_sibling(5 + k // 4).start()
    for n in range(1, 7):
        from_sibling(n).wait_recv()
    for n in range(4):
        for h in range(2):
            poly_to_sibling(h, n).wait_recv()
        add_product(n, near)
    for h in range(2):
        gathers_p[h].arrive(6)
        poly_to_sibling(h, 6).start()
        for n in (4, 5):
            gathers_p[h].arrive(n)
    later(8).wait_recv()
    from_sibling(7).start()
    for h in range(2):
        for n in (4, 5):
            gathers_p[h].arrive_across(n)
            poly_to_sibling(h, n).start()
    for n in (4, 5, 6):
        for h in range(2):
            poly_to_sibling(h, n).wait_recv()
        add_product(n, near)
    from_sibling(7).wait_recv()
    for n in range(7):
        add_product(n, far)
    for h in range(2):
        gathers_p[h].arrive(7)
        gathers_p[h].arrive_across(7)
        poly_to_sibling(h, 7).start()
    for h in range(2):
        poly_to_sibling(h, 7).wait_recv()
    add_product(7, near)
    add_product(7, far)

    product = total[pl.ds(pl.multiple_of(core * 64, 8), TILE)]
    out[...] = (
        math.sqrt(8192) * (coef_linear * ortho[chip_row, core].astype(F32) + product)
    ).astype(BF16)

    for c in across + other_right + [own_left, first_opp] + [later(k) for k in range(9)]:
        c.wait_send()
    for h in range(2):
        gathers_p[h].finish()
        for n in range(8):
            poly_to_sibling(h, n).wait_send()
    for n in range(8):
        from_sibling(n).wait_send()
    for t in range(5):
        for c in half_hops(t, *tasks[t]) + whole_hops(t, *tasks[t]):
            c.wait_send()
    pair_hop(0).wait_send()
    for m in (1, 2, 3):
        pl.when(planes[m] != z_hi)(lambda m=m: pair_hop(m).wait_send())
        pl.when(planes[m] == z_hi)(lambda m=m: all_turned(m).wait_send())
    for m in range(4):
        rows_gathers[m].finish()
        cols_gathers[m].finish()
        for n in range(8):
            cols_to_sibling(m, n).wait_send()


def iterate(blended):
    dma = pltpu.SemaphoreType.DMA
    return pl.pallas_call(
        kernel,
        out_shape=jax.ShapeDtypeStruct((TILE, WIDTH), BF16),
        in_specs=[pl.BlockSpec(memory_space=pltpu.VMEM)],
        out_specs=pl.BlockSpec(memory_space=pltpu.VMEM),
        scratch_shapes=[
            pltpu.VMEM((8, TILE, WIDTH), BF16),
            pltpu.VMEM((8, 2, TILE, WIDTH), BF16),
            pltpu.VMEM((2, 4, TILE, BLOCK), F32),
            pltpu.VMEM((5, 2, 40, BLOCK), F32),
            pltpu.VMEM((5, 2, PIECE, BLOCK), F32),
            pltpu.VMEM((4, PIECE, BLOCK), F32),
            pltpu.VMEM((3, 8, PIECE, 128), BF16),
            pltpu.VMEM((3, 8, PIECE, 128), BF16),
            pltpu.VMEM((WIDTH, BLOCK), BF16),
            pltpu.VMEM((2, 4, 2, 4, PIECE, BLOCK), BF16),
            pltpu.VMEM((8, TILE, BLOCK), BF16),
            pltpu.VMEM((8, 2, 2, 160, BLOCK), BF16),
            pltpu.VMEM((160, BLOCK), F32),
            pltpu.VMEM((384, WIDTH), F32),
            pltpu.VMEM((4, 4, 8, 128), F32),
            dma((6,)), dma((6,)), dma((9,)), dma((9,)), dma((8,)), dma((8,)),
            dma((5, 2)), dma((5, 2)), dma((5, 2)), dma((5, 2)), dma((3,)), dma((3,)), dma((4,)), dma((4,)),
            dma((4, 9)), dma((4, 9)), dma((4, 9)), dma((4, 9)), dma((4, 8)), dma((4, 8)),
            dma((2, 12)), dma((2, 12)), dma((2, 8)), dma((2, 8)),
            dma((4, 3)), dma((4, 3)),
        ],
        compiler_params=pltpu.CompilerParams(
            collective_id=0, has_side_effects=True, vmem_limit_bytes=60 << 20
        ),
    )(blended)


def per_device(grad, momentum):
    new_momentum = momentum_decay * momentum + grad
    blended = (grad + momentum_decay * new_momentum).astype(BF16)
    return (iterate(blended), new_momentum)


def solution(mesh):
    placed = (P("row", "col"), P("row", "col"))
    return jax.shard_map(
        per_device,
        mesh=mesh,
        in_specs=placed,
        out_specs=(P("row", "col"), P("row", "col")),
        check_vma=False,
    )
```

```python
import math

import jax
import jax.numpy as jnp
from jax import lax
from jax.experimental import pallas as pl
from jax.experimental.pallas import tpu as pltpu
from jax.sharding import PartitionSpec as P

momentum_decay = 0.95
target_rms = 0.25
norm_epsilon = 1e-07
coef_linear = 3.4445
coef_cubic = -4.775
coef_quintic = 2.0315

MESH = pl.DeviceIdType.MESH
F32 = jnp.float32
BF16 = jnp.bfloat16

TILE = 320
BLOCK = 640
WIDTH = 1024
PIECE = 80


class Gather:
    def __init__(self, own, whole, some, rows, cut, p, b, right, left, pair, send, recv, across=0, cut_pair=None):
        def copy(n, src, dst, device):
            return pltpu.make_async_remote_copy(
                src, dst, send.at[n], recv.at[n], device_id=device, device_id_type=MESH
            )

        def on(n, p, b, first, size, device):
            place = some(p, b, first, size)
            return copy(n, place, place, device)

        lo, hi = lax.rem(p + 3, 4), lax.rem(p + 1, 4)
        opp = lax.rem(p + 2, 4)
        c = 1 - b
        own_place = whole(p, b)
        around = rows - across
        cut_pair = cut if cut_pair is None else cut_pair
        self.pair = copy(0, own, own_place, pair)
        self.right = copy(1, own, own_place, right)
        self.left = copy(2, own, own_place, left)
        self.right_pair = on(3, p, c, 0, around, right)
        self.left_pair = on(4, p, c, 0, around, left)
        self.on_right = on(5, lo, b, 0, cut, right)
        self.on_left = on(6, hi, b, cut, rows - cut, left)
        self.on_right_pair = on(7, lo, c, 0, cut_pair, right)
        self.on_left_pair = on(8, hi, c, cut_pair, around - cut_pair, left)
        self.all = [
            self.pair, self.right, self.left, self.right_pair, self.left_pair,
            self.on_right, self.on_left, self.on_right_pair, self.on_left_pair,
        ]
        self.across = []
        if across:
            self.across = [on(9 + k, q, b, around, across, pair) for k, q in enumerate((lo, hi, opp))]
            self.all = self.all + self.across
        self.order = [(p, b), (p, c), (lo, b), (hi, b), (lo, c), (hi, c), (opp, b), (opp, c)]

    def start(self):
        self.pair.start()
        self.right.start()
        self.left.start()

    def arrive(self, n):
        waits = {
            1: [self.pair], 2: [self.right], 3: [self.left], 4: [self.right_pair], 5: [self.left_pair],
            6: [self.on_right, self.on_left], 7: [self.on_right_pair, self.on_left_pair],
        }
        starts = {
            1: [self.right_pair, self.left_pair], 2: [self.on_right], 3: [self.on_left],
            4: [self.on_right_pair], 5: [self.on_left_pair],
        }
        if self.across:
            for block, k in ((2, 0), (3, 1), (6, 2)):
                starts[block] = starts.get(block, []) + [self.across[k]]
        for c in waits[n]:
            c.wait_recv()
        for c in starts.get(n, []):
            c.start()

    def arrive_across(self, n):
        if self.across:
            self.across[{4: 0, 5: 1, 7: 2}[n]].wait_recv()

    def finish(self):
        for c in self.all:
            c.wait_send()


def kernel(
    blended, out,
    raw, ortho, part, hop_half, hop_whole, hop_pair, turned, turned_in, spots, gram_cols, gram_rows, poly, square, total, sums,
    b_send, b_recv, l_send, l_recv, bs_send, bs_recv, half_send, half_recv, whole_send, whole_recv, t_send, t_recv, z_send, z_recv,
    gr_send, gr_recv, gc_send, gc_recv, gs_send, gs_recv, p_send, p_recv, ps_send, ps_recv,
    sum_send, sum_recv,
):
    row, col = lax.axis_index("row"), lax.axis_index("col")
    core = lax.rem(row, 2)
    x = lax.rem(lax.div(row, 2), 4)
    z_lo = lax.div(row, 8)
    y, z_hi = lax.div(col, 2), lax.rem(col, 2)
    chip_row = lax.div(row, 2)

    def at(x=x, y=y, z_lo=z_lo, z_hi=z_hi, core=core):
        return ((z_lo * 4 + x) * 2 + core, y * 2 + z_hi)

    def turn(v, n):
        return lax.rem(v + n, 4)

    sibling = at(core=1 - core)
    x_right, x_left = at(x=turn(x, 1)), at(x=turn(x, 3))
    y_right, y_left = at(y=turn(y, 1)), at(y=turn(y, 3))
    lo_pair, hi_pair = at(z_lo=1 - z_lo), at(z_hi=1 - z_hi)
    z = z_hi * 2 + z_lo
    peers = {
        "core": [sibling],
        "x": [at(x=turn(x, n)) for n in (1, 2, 3)],
        "z": [at(z_lo=lax.rem(turn(z, n), 2), z_hi=lax.div(turn(z, n), 2)) for n in (1, 2, 3)],
        "y": [at(y=turn(y, n)) for n in (1, 2, 3)],
    }
    everyone = [d for group in peers.values() for d in group]

    barrier = pltpu.get_barrier_semaphore()
    for d in everyone:
        pl.semaphore_signal(barrier, inc=1, device_id=d, device_id_type=MESH)
    pl.semaphore_wait(barrier, len(everyone))

    lo, hi, opp = turn(x, 3), turn(x, 1), turn(x, 2)
    high = lax.div(x, 2)
    to_opp = high * z_lo + (1 - high) * (1 - z_lo)
    from_opp = (1 - high) * z_lo + high * (1 - z_lo)

    def b_copy(n, b, device, first=0, rows=TILE):
        place = raw.at[b * 4 + x, pl.ds(first, rows)]
        return pltpu.make_async_remote_copy(
            place, place, b_send.at[n], b_recv.at[n], device_id=device, device_id_type=MESH
        )

    across = [b_copy(0, z_lo, lo_pair, 0, 128), b_copy(1, z_lo, lo_pair, 128, 192)]
    own_left = b_copy(2, z_lo, x_left)
    other_right = [b_copy(3, 1 - z_lo, x_right, 0, 128), b_copy(4, 1 - z_lo, x_right, 128, 192)]
    first_opp = b_copy(5, to_opp, at(x=opp))
    order = [
        (x, z_lo), (x, 1 - z_lo), (hi, z_lo), (lo, 1 - z_lo), (opp, from_opp),
        (hi, 1 - z_lo), (lo, z_lo), (opp, 1 - from_opp),
    ]
    raw[z_lo * 4 + x] = blended[...]
    across[0].start()

    mine = jnp.zeros((8, 128), F32)
    for k in range(8):
        wide = blended[:, k * 128 : (k + 1) * 128].astype(F32).reshape(TILE // 8, 8, 128)
        mine = mine + jnp.sum(wide * wide, axis=0)
    for stage, (place, size) in enumerate(((core, 2), (x, 4), (z, 4), (y, 4))):
        group = list(peers.values())[stage]
        sums[stage, place] = mine
        copies = [
            pltpu.make_async_remote_copy(
                sums.at[stage, place], sums.at[stage, place],
                sum_send.at[stage, n], sum_recv.at[stage, n], device_id=d, device_id_type=MESH,
            )
            for n, d in enumerate(group)
        ]
        for c in copies:
            c.start()
        for c in copies:
            c.wait()
        mine = sums[stage, 0]
        for n in range(1, size):
            mine = mine + sums[stage, n]
        if stage == 1:
            own_left.start()
            pl.when(high == 1)(first_opp.start)
        elif stage == 2:
            across[1].start()
    squares_total = jnp.sum(mine, keepdims=True)
    norm_scale = target_rms * math.sqrt(5120) / (jnp.sqrt(squares_total) + norm_epsilon)

    def to_sibling(n, src, send, recv):
        return pltpu.make_async_remote_copy(
            src, src, send.at[n], recv.at[n], device_id=sibling, device_id_type=MESH
        )

    mine_rows = pl.ds(pl.multiple_of(y * PIECE, PIECE), PIECE)

    def scale(src, j):
        def body(k, carry):
            rows = pl.ds(pl.multiple_of(k * 32, 32), 32)
            ortho[j, core, rows] = (src[rows].astype(F32) * norm_scale).astype(BF16)
            return carry

        lax.fori_loop(0, TILE // 32, body, 0)

    def partial(p, b):
        part[b, p] = lax.dot_general(
            ortho[b * 4 + p, core],
            ortho[chip_row].reshape(BLOCK, WIDTH),
            (((1,), (1,)), ((), ())),
            preferred_element_type=F32,
        )

    def half_hops(n, p, b):
        far = turn(y, 2) * PIECE
        return [
            pltpu.make_async_remote_copy(
                part.at[b, p, pl.ds(pl.multiple_of(far + 40 * k, 8), 40)],
                hop_half.at[n, k],
                half_send.at[n, k], half_recv.at[n, k], device_id=d, device_id_type=MESH,
            )
            for k, d in enumerate((y_right, y_left))
        ]

    def whole_hops(n, p, b):
        return [
            pltpu.make_async_remote_copy(
                part.at[b, p, pl.ds(pl.multiple_of(near * PIECE, 8), PIECE)],
                hop_whole.at[n, k],
                whole_send.at[n, k], whole_recv.at[n, k], device_id=d, device_id_type=MESH,
            )
            for k, (near, d) in enumerate(((turn(y, 1), y_right), (turn(y, 3), y_left)))
        ]

    places = (x, lo, hi, opp)

    planes = (None, 1 - z_lo, z_lo, from_opp)

    tasks = ((x, z_lo), (x, 1 - z_lo), (lo, 1 - z_lo), (hi, z_lo), (opp, from_opp))

    def reduce_1(t):
        partial(*tasks[t])
        for c in half_hops(t, *tasks[t]):
            c.start()

    def reduce_2(t):
        p, b = tasks[t]
        halves, wholes = half_hops(t, p, b), whole_hops(t, p, b)
        for k, near in enumerate((turn(y, 1), turn(y, 3))):
            halves[k].wait_recv()
            rows = pl.ds(pl.multiple_of(near * PIECE + 40 * k, 8), 40)
            part[b, p, rows] = part[b, p, rows] + hop_half[t, k]
            wholes[k].start()

    def reduce_3(t):
        p, b = tasks[t]
        for c in whole_hops(t, p, b):
            c.wait_recv()
        part[b, p, mine_rows] = part[b, p, mine_rows] + (hop_whole[t, 0] + hop_whole[t, 1])

    def pair_hop(m):
        b = 1 - z_hi if m == 0 else planes[m]
        return pltpu.make_async_remote_copy(
            part.at[b, places[m], mine_rows], hop_pair.at[m],
            z_send.at[m], z_recv.at[m], device_id=hi_pair, device_id_type=MESH,
        )

    def reduce_4(m):
        if m == 0:
            pair_hop(0).start()
        else:
            pl.when(planes[m] != z_hi)(lambda: pair_hop(m).start())

    def keep(m, tile):
        p = places[m]
        gram_cols[z_hi, p, core, y] = tile
        gram_rows[chip_row, pl.ds(pl.multiple_of(p * PIECE, 16), PIECE)] = tile

    def summed(m):
        pair_hop(m).wait_recv()
        return part[z_hi, places[m], mine_rows] + hop_pair[m]

    def turned_pieces(m):
        away = (0, 2, 1, 3)[m]
        return [
            pltpu.make_async_remote_copy(
                turned.at[m - 1, a * 4 + k], turned_in.at[away - 1, core * 4 + y],
                t_send.at[m - 1], t_recv.at[away - 1],
                device_id=((z_hi * 4 + places[m]) * 2 + a, k * 2 + z_lo), device_id_type=MESH,
            )
            for a in range(2) for k in range(4)
        ]

    def all_turned(m):
        return pltpu.make_async_remote_copy(
            turned.at[m - 1], turned_in.at[m - 1],
            t_send.at[m - 1], t_recv.at[m - 1], device_id=sibling, device_id_type=MESH,
        )

    def reduce_5(m):
        @pl.when(planes[m] == z_hi)
        def _():
            tile = summed(m)
            keep(m, tile.astype(BF16))
            tall = jnp.concatenate([tile, jnp.zeros((128 - PIECE, BLOCK), F32)], axis=0).T
            turned[m - 1] = tall.astype(BF16).reshape(8, PIECE, 128)
            for c in turned_pieces(m):
                c.start()

    def finish_tile(m):
        if m == 0:
            keep(0, summed(0).astype(BF16))
            return

        @pl.when(planes[m] != z_hi)
        def _():
            all_turned(m).wait_recv()
            wide = jnp.concatenate([turned_in[m - 1, k] for k in range(8)], axis=1)
            keep(m, jnp.dot(wide, spots[...], preferred_element_type=F32).astype(BF16))

    def from_sibling(n):
        p, b = order[n]
        return to_sibling(n, ortho.at[b * 4 + p, core], bs_send, bs_recv)

    def later(k):
        if k == 8:
            place = ortho.at[(1 - to_opp) * 4 + x, core]
            return pltpu.make_async_remote_copy(
                place, place, l_send.at[8], l_recv.at[8], device_id=at(x=opp), device_id_type=MESH
            )
        p, b = (x, 1 - z_lo if k < 4 else z_lo)
        place = ortho.at[b * 4 + p, core, pl.ds(k % 4 * 80, 80)]
        return pltpu.make_async_remote_copy(
            place, place, l_send.at[k], l_recv.at[k],
                device_id=x_left if k < 4 else x_right, device_id_type=MESH
        )

    def process(n):
        p, b = order[n]
        scale(raw.at[b * 4 + p], b * 4 + p)
        from_sibling(n).start()
        if n == 0:
            from_sibling(0).wait_recv()

    def gather_rows(m):
        def place(p, b, first, rows):
            part_of = turn(p, (0, 3, 1, 2)[m]) * PIECE
            return gram_rows.at[b * 4 + p, pl.ds(pl.multiple_of(part_of + first, 16), rows)]

        return Gather(
            place(x, z_lo, 0, PIECE), lambda p, b: place(p, b, 0, PIECE), place,
            PIECE, 48, x, z_lo, x_right, x_left, lo_pair, gr_send.at[m], gr_recv.at[m],
        )

    def gather_cols(m):
        q = turn(x, (0, 3, 1, 2)[m])

        def place(p, b, first, rows):
            return gram_cols.at[b, q, core, p, pl.ds(first, rows)]

        return Gather(
            place(y, z_hi, 0, PIECE), lambda p, b: place(p, b, 0, PIECE), place,
            PIECE, 48, y, z_hi, y_right, y_left, hi_pair, gc_send.at[m], gc_recv.at[m],
        )

    def cols_to_sibling(m, n):
        p, b = cols_gathers[m].order[n]
        place = gram_cols.at[b, turn(x, (0, 3, 1, 2)[m]), core, p]
        return to_sibling(n, place, gs_send.at[m], gs_recv.at[m])

    rows_gathers = [gather_rows(m) for m in range(4)]
    cols_gathers = [gather_cols(m) for m in range(4)]

    def spread(m, event):
        if event == 0:
            finish_tile(m)
            cols_gathers[m].start()
            rows_gathers[m].start()
            cols_to_sibling(m, 0).start()
        for n in ((), (1, 2, 3), (4, 5), (6, 7))[event]:
            cols_gathers[m].arrive(n)
            cols_to_sibling(m, n).start()
            rows_gathers[m].arrive(n)

    spot = lax.broadcasted_iota(jnp.int32, (WIDTH, BLOCK), 0)
    column = lax.broadcasted_iota(jnp.int32, (WIDTH, BLOCK), 1)
    lane = spot % 128
    spots[...] = jnp.where((lane < PIECE) & (column == spot // 128 * PIECE + lane), 1.0, 0.0).astype(BF16)

    across[0].wait_recv()
    other_right[0].start()
    process(0)
    reduce_1(0)
    across[1].wait_recv()
    other_right[1].start()
    pl.when(high == 0)(first_opp.start)
    process(1)
    reduce_1(1)
    reduce_2(0)
    own_left.wait_recv()
    process(2)
    reduce_1(3)
    reduce_2(1)
    reduce_3(0)
    reduce_2(3)
    reduce_3(1)
    reduce_4(0)
    for c in other_right:
        c.wait_recv()
    process(3)
    reduce_1(2)
    reduce_3(3)
    reduce_4(2)
    later(0).start()
    later(4).start()
    later(1).start()
    later(5).start()
    first_opp.wait_recv()
    process(4)
    reduce_1(4)
    spread(0, 0)
    reduce_2(2)
    reduce_5(2)
    reduce_2(4)
    later(2).start()
    later(6).start()
    spread(0, 1)
    later(3).start()
    later(7).start()
    reduce_3(2)
    reduce_4(1)
    reduce_3(4)
    reduce_4(3)
    spread(0, 2)
    reduce_5(1)
    spread(1, 0)
    reduce_5(3)
    spread(2, 0)
    spread(0, 3)
    spread(1, 1)
    spread(3, 0)
    spread(2, 1)
    spread(1, 2)
    spread(3, 1)
    spread(2, 2)
    spread(3, 2)
    spread(1, 3)
    spread(2, 3)
    spread(3, 3)
    for m in range(4):
        for n in range(8):
            cols_to_sibling(m, n).wait_recv()

    def half_of_poly(h):
        rows = pl.ds(h * 160, 160)
        square[...] = jnp.zeros_like(square)

        def add_square(k, carry):
            right = gram_cols[lax.div(k, 4), lax.rem(k, 4)].reshape(BLOCK, BLOCK)
            square[...] += jnp.dot(gram_rows[k, rows], right, preferred_element_type=F32)
            return carry

        lax.fori_loop(0, 8, add_square, 0)
        poly[col, h, core] = (
            coef_cubic * gram_rows[chip_row, rows].astype(F32) + coef_quintic * square[...]
        ).astype(BF16)

    gathers_p = [
        Gather(
            poly.at[col, h, core],
            lambda p, b, h=h: poly.at[p * 2 + b, h, core],
            lambda p, b, first, rows, h=h: poly.at[p * 2 + b, h, core, pl.ds(first, rows)],
            160, 80, y, z_hi, y_right, y_left, hi_pair, p_send.at[h], p_recv.at[h], across=64, cut_pair=48,
        )
        for h in range(2)
    ]

    def poly_to_sibling(h, n):
        p, b = gathers_p[h].order[n]
        return to_sibling(n, poly.at[p * 2 + b, h, core], ps_send.at[h], ps_recv.at[h])

    later(8).start()
    for h in range(2):
        half_of_poly(h)
        gathers_p[h].start()
        poly_to_sibling(h, 0).start()

    lanes = pl.ds(pl.multiple_of(core * 256, 128), 384)
    total[...] = jnp.zeros_like(total)

    def add_product(n, columns):
        p, b = gathers_p[0].order[n]
        first = pl.multiple_of(p * PIECE, 16)
        left = [
            poly[p * 2 + b, lax.div(q, 2), a, pl.ds(pl.multiple_of(lax.rem(q, 2) * PIECE, 16), PIECE), lanes]
            for q in columns for a in range(2)
        ]
        right = [ortho[b * 4 + q, a, pl.ds(first, PIECE)] for q in columns for a in range(2)]
        total[...] += lax.dot_general(
            jnp.concatenate(left, axis=0), jnp.concatenate(right, axis=0),
            (((0,), (0,)), ((), ())), preferred_element_type=F32,
        )

    near, far = (x, hi), (lo, opp)

    for h in range(2):
        for n in (1, 2, 3):
            gathers_p[h].arrive(n)
            poly_to_sibling(h, n).start()
    for k in range(8):
        later(k).wait_recv()
        if k % 4 == 3:
            from_sibling(5 + k // 4).start()
    for n in range(1, 7):
        from_sibling(n).wait_recv()
    for n in range(4):
        for h in range(2):
            poly_to_sibling(h, n).wait_recv()
        add_product(n, near)
    for h in range(2):
        gathers_p[h].arrive(6)
        poly_to_sibling(h, 6).start()
        for n in (4, 5):
            gathers_p[h].arrive(n)
    later(8).wait_recv()
    from_sibling(7).start()
    for h in range(2):
        for n in (4, 5):
            gathers_p[h].arrive_across(n)
            poly_to_sibling(h, n).start()
    for n in (4, 5, 6):
        for h in range(2):
            poly_to_sibling(h, n).wait_recv()
        add_product(n, near)
    from_sibling(7).wait_recv()
    for n in range(7):
        add_product(n, far)
    for h in range(2):
        gathers_p[h].arrive(7)
        gathers_p[h].arrive_across(7)
        poly_to_sibling(h, 7).start()
    for h in range(2):
        poly_to_sibling(h, 7).wait_recv()
    add_product(7, near)
    add_product(7, far)

    product = total[pl.ds(pl.multiple_of(core * 64, 8), TILE)]
    out[...] = (
        math.sqrt(8192) * (coef_linear * ortho[chip_row, core].astype(F32) + product)
    ).astype(BF16)

    for c in across + other_right + [own_left, first_opp] + [later(k) for k in range(9)]:
        c.wait_send()
    for h in range(2):
        gathers_p[h].finish()
        for n in range(8):
            poly_to_sibling(h, n).wait_send()
    for n in range(8):
        from_sibling(n).wait_send()
    for t in range(5):
        for c in half_hops(t, *tasks[t]) + whole_hops(t, *tasks[t]):
            c.wait_send()
    pair_hop(0).wait_send()
    for m in (1, 2, 3):
        pl.when(planes[m] != z_hi)(lambda m=m: pair_hop(m).wait_send())
        pl.when(planes[m] == z_hi)(lambda m=m: all_turned(m).wait_send())
    for m in range(4):
        rows_gathers[m].finish()
        cols_gathers[m].finish()
        for n in range(8):
            cols_to_sibling(m, n).wait_send()


def iterate(blended):
    dma = pltpu.SemaphoreType.DMA
    return pl.pallas_call(
        kernel,
        out_shape=jax.ShapeDtypeStruct((TILE, WIDTH), BF16),
        in_specs=[pl.BlockSpec(memory_space=pltpu.VMEM)],
        out_specs=pl.BlockSpec(memory_space=pltpu.VMEM),
        scratch_shapes=[
            pltpu.VMEM((8, TILE, WIDTH), BF16),
            pltpu.VMEM((8, 2, TILE, WIDTH), BF16),
            pltpu.VMEM((2, 4, TILE, BLOCK), F32),
            pltpu.VMEM((5, 2, 40, BLOCK), F32),
            pltpu.VMEM((5, 2, PIECE, BLOCK), F32),
            pltpu.VMEM((4, PIECE, BLOCK), F32),
            pltpu.VMEM((3, 8, PIECE, 128), BF16),
            pltpu.VMEM((3, 8, PIECE, 128), BF16),
            pltpu.VMEM((WIDTH, BLOCK), BF16),
            pltpu.VMEM((2, 4, 2, 4, PIECE, BLOCK), BF16),
            pltpu.VMEM((8, TILE, BLOCK), BF16),
            pltpu.VMEM((8, 2, 2, 160, BLOCK), BF16),
            pltpu.VMEM((160, BLOCK), F32),
            pltpu.VMEM((384, WIDTH), F32),
            pltpu.VMEM((4, 4, 8, 128), F32),
            dma((6,)), dma((6,)), dma((9,)), dma((9,)), dma((8,)), dma((8,)),
            dma((5, 2)), dma((5, 2)), dma((5, 2)), dma((5, 2)), dma((3,)), dma((3,)), dma((4,)), dma((4,)),
            dma((4, 9)), dma((4, 9)), dma((4, 9)), dma((4, 9)), dma((4, 8)), dma((4, 8)),
            dma((2, 12)), dma((2, 12)), dma((2, 8)), dma((2, 8)),
            dma((4, 3)), dma((4, 3)),
        ],
        compiler_params=pltpu.CompilerParams(
            collective_id=0, has_side_effects=True, vmem_limit_bytes=60 << 20
        ),
    )(blended)


def per_device(grad, momentum):
    new_momentum = momentum_decay * momentum + grad
    blended = (grad + momentum_decay * new_momentum).astype(BF16)
    return (iterate(blended), new_momentum)


def solution(mesh):
    placed = (P("row", "col"), P("row", "col"))
    return jax.shard_map(
        per_device,
        mesh=mesh,
        in_specs=placed,
        out_specs=(P("row", "col"), P("row", "col")),
        check_vma=False,
    )
```

```python
import math

import jax
import jax.numpy as jnp
from jax import lax
from jax.experimental import pallas as pl
from jax.experimental.pallas import tpu as pltpu
from jax.sharding import PartitionSpec as P

momentum_decay = 0.95
target_rms = 0.25
norm_epsilon = 1e-07
coef_linear = 3.4445
coef_cubic = -4.775
coef_quintic = 2.0315

MESH = pl.DeviceIdType.MESH
F32 = jnp.float32
BF16 = jnp.bfloat16

TILE = 320
BLOCK = 640
WIDTH = 1024
PIECE = 80


class Gather:
    def __init__(self, own, whole, some, rows, cut, p, b, right, left, pair, send, recv, across=0, cut_pair=None):
        def copy(n, src, dst, device):
            return pltpu.make_async_remote_copy(
                src, dst, send.at[n], recv.at[n], device_id=device, device_id_type=MESH
            )

        def on(n, p, b, first, size, device):
            place = some(p, b, first, size)
            return copy(n, place, place, device)

        lo, hi = lax.rem(p + 3, 4), lax.rem(p + 1, 4)
        opp = lax.rem(p + 2, 4)
        c = 1 - b
        own_place = whole(p, b)
        around = rows - across
        cut_pair = cut if cut_pair is None else cut_pair
        self.pair = copy(0, own, own_place, pair)
        self.right = copy(1, own, own_place, right)
        self.left = copy(2, own, own_place, left)
        self.right_pair = on(3, p, c, 0, around, right)
        self.left_pair = on(4, p, c, 0, around, left)
        self.on_right = on(5, lo, b, 0, cut, right)
        self.on_left = on(6, hi, b, cut, rows - cut, left)
        self.on_right_pair = on(7, lo, c, 0, cut_pair, right)
        self.on_left_pair = on(8, hi, c, cut_pair, around - cut_pair, left)
        self.all = [
            self.pair, self.right, self.left, self.right_pair, self.left_pair,
            self.on_right, self.on_left, self.on_right_pair, self.on_left_pair,
        ]
        self.across = []
        if across:
            self.across = [on(9 + k, q, b, around, across, pair) for k, q in enumerate((lo, hi, opp))]
            self.all = self.all + self.across
        self.order = [(p, b), (p, c), (lo, b), (hi, b), (lo, c), (hi, c), (opp, b), (opp, c)]

    def start(self):
        self.pair.start()
        self.right.start()
        self.left.start()

    def arrive(self, n):
        waits = {
            1: [self.pair], 2: [self.right], 3: [self.left], 4: [self.right_pair], 5: [self.left_pair],
            6: [self.on_right, self.on_left], 7: [self.on_right_pair, self.on_left_pair],
        }
        starts = {
            1: [self.right_pair, self.left_pair], 2: [self.on_right], 3: [self.on_left],
            4: [self.on_right_pair], 5: [self.on_left_pair],
        }
        if self.across:
            for block, k in ((2, 0), (3, 1), (6, 2)):
                starts[block] = starts.get(block, []) + [self.across[k]]
        for c in waits[n]:
            c.wait_recv()
        for c in starts.get(n, []):
            c.start()

    def arrive_across(self, n):
        if self.across:
            self.across[{4: 0, 5: 1, 7: 2}[n]].wait_recv()

    def finish(self):
        for c in self.all:
            c.wait_send()


def kernel(
    blended, out,
    raw, ortho, part, hop_half, hop_whole, hop_pair, turned, turned_in, spots, gram_cols, gram_rows, poly, square, total, sums,
    b_send, b_recv, l_send, l_recv, bs_send, bs_recv, half_send, half_recv, whole_send, whole_recv, t_send, t_recv, z_send, z_recv,
    gr_send, gr_recv, gc_send, gc_recv, gs_send, gs_recv, p_send, p_recv, ps_send, ps_recv,
    sum_send, sum_recv,
):
    row, col = lax.axis_index("row"), lax.axis_index("col")
    core = lax.rem(row, 2)
    x = lax.rem(lax.div(row, 2), 4)
    z_lo = lax.div(row, 8)
    y, z_hi = lax.div(col, 2), lax.rem(col, 2)
    chip_row = lax.div(row, 2)

    def at(x=x, y=y, z_lo=z_lo, z_hi=z_hi, core=core):
        return ((z_lo * 4 + x) * 2 + core, y * 2 + z_hi)

    def turn(v, n):
        return lax.rem(v + n, 4)

    sibling = at(core=1 - core)
    x_right, x_left = at(x=turn(x, 1)), at(x=turn(x, 3))
    y_right, y_left = at(y=turn(y, 1)), at(y=turn(y, 3))
    lo_pair, hi_pair = at(z_lo=1 - z_lo), at(z_hi=1 - z_hi)
    z = z_hi * 2 + z_lo
    peers = {
        "core": [sibling],
        "x": [at(x=turn(x, n)) for n in (1, 2, 3)],
        "z": [at(z_lo=lax.rem(turn(z, n), 2), z_hi=lax.div(turn(z, n), 2)) for n in (1, 2, 3)],
        "y": [at(y=turn(y, n)) for n in (1, 2, 3)],
    }
    everyone = [d for group in peers.values() for d in group]

    barrier = pltpu.get_barrier_semaphore()
    for d in everyone:
        pl.semaphore_signal(barrier, inc=1, device_id=d, device_id_type=MESH)
    pl.semaphore_wait(barrier, len(everyone))

    lo, hi, opp = turn(x, 3), turn(x, 1), turn(x, 2)
    high = lax.div(x, 2)
    to_opp = high * z_lo + (1 - high) * (1 - z_lo)
    from_opp = (1 - high) * z_lo + high * (1 - z_lo)

    def b_copy(n, b, device, first=0, rows=TILE):
        place = raw.at[b * 4 + x, pl.ds(first, rows)]
        return pltpu.make_async_remote_copy(
            place, place, b_send.at[n], b_recv.at[n], device_id=device, device_id_type=MESH
        )

    across = [b_copy(0, z_lo, lo_pair, 0, 128), b_copy(1, z_lo, lo_pair, 128, 192)]
    own_left = b_copy(2, z_lo, x_left)
    other_right = [b_copy(3, 1 - z_lo, x_right, 0, 128), b_copy(4, 1 - z_lo, x_right, 128, 192)]
    first_opp = b_copy(5, to_opp, at(x=opp))
    order = [
        (x, z_lo), (x, 1 - z_lo), (hi, z_lo), (lo, 1 - z_lo), (opp, from_opp),
        (hi, 1 - z_lo), (lo, z_lo), (opp, 1 - from_opp),
    ]
    raw[z_lo * 4 + x] = blended[...]
    across[0].start()

    mine = jnp.zeros((8, 128), F32)
    for k in range(8):
        wide = blended[:, k * 128 : (k + 1) * 128].astype(F32).reshape(TILE // 8, 8, 128)
        mine = mine + jnp.sum(wide * wide, axis=0)
    for stage, (place, size) in enumerate(((core, 2), (x, 4), (z, 4), (y, 4))):
        group = list(peers.values())[stage]
        sums[stage, place] = mine
        copies = [
            pltpu.make_async_remote_copy(
                sums.at[stage, place], sums.at[stage, place],
                sum_send.at[stage, n], sum_recv.at[stage, n], device_id=d, device_id_type=MESH,
            )
            for n, d in enumerate(group)
        ]
        for c in copies:
            c.start()
        for c in copies:
            c.wait()
        mine = sums[stage, 0]
        for n in range(1, size):
            mine = mine + sums[stage, n]
        if stage == 1:
            own_left.start()
            pl.when(high == 1)(first_opp.start)
        elif stage == 2:
            across[1].start()
            across[0].wait_recv()
            other_right[0].start()
    squares_total = jnp.sum(mine, keepdims=True)
    norm_scale = target_rms * math.sqrt(5120) / (jnp.sqrt(squares_total) + norm_epsilon)

    def to_sibling(n, src, send, recv):
        return pltpu.make_async_remote_copy(
            src, src, send.at[n], recv.at[n], device_id=sibling, device_id_type=MESH
        )

    mine_rows = pl.ds(pl.multiple_of(y * PIECE, PIECE), PIECE)

    def scale(src, j):
        def body(k, carry):
            rows = pl.ds(pl.multiple_of(k * 32, 32), 32)
            ortho[j, core, rows] = (src[rows].astype(F32) * norm_scale).astype(BF16)
            return carry

        lax.fori_loop(0, TILE // 32, body, 0)

    def partial(p, b):
        part[b, p] = lax.dot_general(
            ortho[b * 4 + p, core],
            ortho[chip_row].reshape(BLOCK, WIDTH),
            (((1,), (1,)), ((), ())),
            preferred_element_type=F32,
        )

    def half_hops(n, p, b):
        far = turn(y, 2) * PIECE
        return [
            pltpu.make_async_remote_copy(
                part.at[b, p, pl.ds(pl.multiple_of(far + 40 * k, 8), 40)],
                hop_half.at[n, k],
                half_send.at[n, k], half_recv.at[n, k], device_id=d, device_id_type=MESH,
            )
            for k, d in enumerate((y_right, y_left))
        ]

    def whole_hops(n, p, b):
        return [
            pltpu.make_async_remote_copy(
                part.at[b, p, pl.ds(pl.multiple_of(near * PIECE, 8), PIECE)],
                hop_whole.at[n, k],
                whole_send.at[n, k], whole_recv.at[n, k], device_id=d, device_id_type=MESH,
            )
            for k, (near, d) in enumerate(((turn(y, 1), y_right), (turn(y, 3), y_left)))
        ]

    places = (x, lo, hi, opp)

    planes = (None, 1 - z_lo, z_lo, from_opp)

    tasks = ((x, z_lo), (x, 1 - z_lo), (lo, 1 - z_lo), (hi, z_lo), (opp, from_opp))

    def reduce_1(t):
        partial(*tasks[t])
        for c in half_hops(t, *tasks[t]):
            c.start()

    def reduce_2(t):
        p, b = tasks[t]
        halves, wholes = half_hops(t, p, b), whole_hops(t, p, b)
        for k, near in enumerate((turn(y, 1), turn(y, 3))):
            halves[k].wait_recv()
            rows = pl.ds(pl.multiple_of(near * PIECE + 40 * k, 8), 40)
            part[b, p, rows] = part[b, p, rows] + hop_half[t, k]
            wholes[k].start()

    def reduce_3(t):
        p, b = tasks[t]
        for c in whole_hops(t, p, b):
            c.wait_recv()
        part[b, p, mine_rows] = part[b, p, mine_rows] + (hop_whole[t, 0] + hop_whole[t, 1])

    def pair_hop(m):
        b = 1 - z_hi if m == 0 else planes[m]
        return pltpu.make_async_remote_copy(
            part.at[b, places[m], mine_rows], hop_pair.at[m],
            z_send.at[m], z_recv.at[m], device_id=hi_pair, device_id_type=MESH,
        )

    def reduce_4(m):
        if m == 0:
            pair_hop(0).start()
        else:
            pl.when(planes[m] != z_hi)(lambda: pair_hop(m).start())

    def keep(m, tile):
        p = places[m]
        gram_cols[z_hi, p, core, y] = tile
        gram_rows[chip_row, pl.ds(pl.multiple_of(p * PIECE, 16), PIECE)] = tile

    def summed(m):
        pair_hop(m).wait_recv()
        return part[z_hi, places[m], mine_rows] + hop_pair[m]

    def turned_pieces(m):
        away = (0, 2, 1, 3)[m]
        return [
            pltpu.make_async_remote_copy(
                turned.at[m - 1, a * 4 + k], turned_in.at[away - 1, core * 4 + y],
                t_send.at[m - 1], t_recv.at[away - 1],
                device_id=((z_hi * 4 + places[m]) * 2 + a, k * 2 + z_lo), device_id_type=MESH,
            )
            for a in range(2) for k in range(4)
        ]

    def all_turned(m):
        return pltpu.make_async_remote_copy(
            turned.at[m - 1], turned_in.at[m - 1],
            t_send.at[m - 1], t_recv.at[m - 1], device_id=sibling, device_id_type=MESH,
        )

    def reduce_5(m):
        @pl.when(planes[m] == z_hi)
        def _():
            tile = summed(m)
            keep(m, tile.astype(BF16))
            tall = jnp.concatenate([tile, jnp.zeros((128 - PIECE, BLOCK), F32)], axis=0).T
            turned[m - 1] = tall.astype(BF16).reshape(8, PIECE, 128)
            for c in turned_pieces(m):
                c.start()

    def finish_tile(m):
        if m == 0:
            keep(0, summed(0).astype(BF16))
            return

        @pl.when(planes[m] != z_hi)
        def _():
            all_turned(m).wait_recv()
            wide = jnp.concatenate([turned_in[m - 1, k] for k in range(8)], axis=1)
            keep(m, jnp.dot(wide, spots[...], preferred_element_type=F32).astype(BF16))

    def from_sibling(n):
        p, b = order[n]
        return to_sibling(n, ortho.at[b * 4 + p, core], bs_send, bs_recv)

    def later(k):
        if k == 8:
            place = ortho.at[(1 - to_opp) * 4 + x, core]
            return pltpu.make_async_remote_copy(
                place, place, l_send.at[8], l_recv.at[8], device_id=at(x=opp), device_id_type=MESH
            )
        p, b = (x, 1 - z_lo if k < 4 else z_lo)
        place = ortho.at[b * 4 + p, core, pl.ds(k % 4 * 80, 80)]
        return pltpu.make_async_remote_copy(
            place, place, l_send.at[k], l_recv.at[k],
                device_id=x_left if k < 4 else x_right, device_id_type=MESH
        )

    def process(n):
        p, b = order[n]
        scale(raw.at[b * 4 + p], b * 4 + p)
        from_sibling(n).start()
        if n == 0:
            from_sibling(0).wait_recv()

    def gather_rows(m):
        def place(p, b, first, rows):
            part_of = turn(p, (0, 3, 1, 2)[m]) * PIECE
            return gram_rows.at[b * 4 + p, pl.ds(pl.multiple_of(part_of + first, 16), rows)]

        return Gather(
            place(x, z_lo, 0, PIECE), lambda p, b: place(p, b, 0, PIECE), place,
            PIECE, 48, x, z_lo, x_right, x_left, lo_pair, gr_send.at[m], gr_recv.at[m],
        )

    def gather_cols(m):
        q = turn(x, (0, 3, 1, 2)[m])

        def place(p, b, first, rows):
            return gram_cols.at[b, q, core, p, pl.ds(first, rows)]

        return Gather(
            place(y, z_hi, 0, PIECE), lambda p, b: place(p, b, 0, PIECE), place,
            PIECE, 48, y, z_hi, y_right, y_left, hi_pair, gc_send.at[m], gc_recv.at[m],
        )

    def cols_to_sibling(m, n):
        p, b = cols_gathers[m].order[n]
        place = gram_cols.at[b, turn(x, (0, 3, 1, 2)[m]), core, p]
        return to_sibling(n, place, gs_send.at[m], gs_recv.at[m])

    rows_gathers = [gather_rows(m) for m in range(4)]
    cols_gathers = [gather_cols(m) for m in range(4)]

    def spread(m, event):
        if event == 0:
            finish_tile(m)
            cols_gathers[m].start()
            rows_gathers[m].start()
            cols_to_sibling(m, 0).start()
        for n in ((), (1, 2, 3), (4, 5), (6, 7))[event]:
            cols_gathers[m].arrive(n)
            cols_to_sibling(m, n).start()
            rows_gathers[m].arrive(n)

    spot = lax.broadcasted_iota(jnp.int32, (WIDTH, BLOCK), 0)
    column = lax.broadcasted_iota(jnp.int32, (WIDTH, BLOCK), 1)
    lane = spot % 128
    spots[...] = jnp.where((lane < PIECE) & (column == spot // 128 * PIECE + lane), 1.0, 0.0).astype(BF16)

    process(0)
    reduce_1(0)
    across[1].wait_recv()
    other_right[1].start()
    pl.when(high == 0)(first_opp.start)
    process(1)
    reduce_1(1)
    reduce_2(0)
    own_left.wait_recv()
    process(2)
    reduce_1(3)
    reduce_2(1)
    reduce_3(0)
    reduce_2(3)
    reduce_3(1)
    reduce_4(0)
    for c in other_right:
        c.wait_recv()
    process(3)
    reduce_1(2)
    later(0).start()
    later(4).start()
    reduce_3(3)
    reduce_4(2)
    later(1).start()
    later(5).start()
    first_opp.wait_recv()
    process(4)
    reduce_1(4)
    spread(0, 0)
    reduce_2(2)
    reduce_5(2)
    reduce_2(4)
    later(2).start()
    later(6).start()
    spread(0, 1)
    later(3).start()
    later(7).start()
    reduce_3(2)
    reduce_4(1)
    reduce_3(4)
    reduce_4(3)
    spread(0, 2)
    reduce_5(1)
    spread(1, 0)
    reduce_5(3)
    spread(2, 0)
    spread(0, 3)
    spread(1, 1)
    spread(3, 0)
    spread(2, 1)
    spread(1, 2)
    spread(3, 1)
    spread(2, 2)
    spread(3, 2)
    spread(1, 3)
    spread(2, 3)
    spread(3, 3)
    for m in range(4):
        for n in range(8):
            cols_to_sibling(m, n).wait_recv()

    def half_of_poly(h):
        rows = pl.ds(h * 160, 160)
        square[...] = jnp.zeros_like(square)

        def add_square(k, carry):
            right = gram_cols[lax.div(k, 4), lax.rem(k, 4)].reshape(BLOCK, BLOCK)
            square[...] += jnp.dot(gram_rows[k, rows], right, preferred_element_type=F32)
            return carry

        lax.fori_loop(0, 8, add_square, 0)
        poly[col, h, core] = (
            coef_cubic * gram_rows[chip_row, rows].astype(F32) + coef_quintic * square[...]
        ).astype(BF16)

    gathers_p = [
        Gather(
            poly.at[col, h, core],
            lambda p, b, h=h: poly.at[p * 2 + b, h, core],
            lambda p, b, first, rows, h=h: poly.at[p * 2 + b, h, core, pl.ds(first, rows)],
            160, 80, y, z_hi, y_right, y_left, hi_pair, p_send.at[h], p_recv.at[h], across=64, cut_pair=48,
        )
        for h in range(2)
    ]

    def poly_to_sibling(h, n):
        p, b = gathers_p[h].order[n]
        return to_sibling(n, poly.at[p * 2 + b, h, core], ps_send.at[h], ps_recv.at[h])

    later(8).start()
    for h in range(2):
        half_of_poly(h)
        gathers_p[h].start()
        poly_to_sibling(h, 0).start()

    lanes = pl.ds(pl.multiple_of(core * 256, 128), 384)
    total[...] = jnp.zeros_like(total)

    def add_product(n, columns):
        p, b = gathers_p[0].order[n]
        first = pl.multiple_of(p * PIECE, 16)
        left = [
            poly[p * 2 + b, lax.div(q, 2), a, pl.ds(pl.multiple_of(lax.rem(q, 2) * PIECE, 16), PIECE), lanes]
            for q in columns for a in range(2)
        ]
        right = [ortho[b * 4 + q, a, pl.ds(first, PIECE)] for q in columns for a in range(2)]
        total[...] += lax.dot_general(
            jnp.concatenate(left, axis=0), jnp.concatenate(right, axis=0),
            (((0,), (0,)), ((), ())), preferred_element_type=F32,
        )

    near, far = (x, hi), (lo, opp)

    for h in range(2):
        for n in (1, 2, 3):
            gathers_p[h].arrive(n)
            poly_to_sibling(h, n).start()
    for k in range(8):
        later(k).wait_recv()
        if k % 4 == 3:
            from_sibling(5 + k // 4).start()
    for n in range(1, 7):
        from_sibling(n).wait_recv()
    for n in range(4):
        for h in range(2):
            poly_to_sibling(h, n).wait_recv()
        add_product(n, near)
    for h in range(2):
        gathers_p[h].arrive(6)
        poly_to_sibling(h, 6).start()
        for n in (4, 5):
            gathers_p[h].arrive(n)
    later(8).wait_recv()
    from_sibling(7).start()
    for h in range(2):
        for n in (4, 5):
            gathers_p[h].arrive_across(n)
            poly_to_sibling(h, n).start()
    for n in (4, 5, 6):
        for h in range(2):
            poly_to_sibling(h, n).wait_recv()
        add_product(n, near)
    from_sibling(7).wait_recv()
    for n in range(7):
        add_product(n, far)
    for h in range(2):
        gathers_p[h].arrive(7)
        gathers_p[h].arrive_across(7)
        poly_to_sibling(h, 7).start()
    for h in range(2):
        poly_to_sibling(h, 7).wait_recv()
    add_product(7, near)
    add_product(7, far)

    product = total[pl.ds(pl.multiple_of(core * 64, 8), TILE)]
    out[...] = (
        math.sqrt(8192) * (coef_linear * ortho[chip_row, core].astype(F32) + product)
    ).astype(BF16)

    for c in across + other_right + [own_left, first_opp] + [later(k) for k in range(9)]:
        c.wait_send()
    for h in range(2):
        gathers_p[h].finish()
        for n in range(8):
            poly_to_sibling(h, n).wait_send()
    for n in range(8):
        from_sibling(n).wait_send()
    for t in range(5):
        for c in half_hops(t, *tasks[t]) + whole_hops(t, *tasks[t]):
            c.wait_send()
    pair_hop(0).wait_send()
    for m in (1, 2, 3):
        pl.when(planes[m] != z_hi)(lambda m=m: pair_hop(m).wait_send())
        pl.when(planes[m] == z_hi)(lambda m=m: all_turned(m).wait_send())
    for m in range(4):
        rows_gathers[m].finish()
        cols_gathers[m].finish()
        for n in range(8):
            cols_to_sibling(m, n).wait_send()


def iterate(blended):
    dma = pltpu.SemaphoreType.DMA
    return pl.pallas_call(
        kernel,
        out_shape=jax.ShapeDtypeStruct((TILE, WIDTH), BF16),
        in_specs=[pl.BlockSpec(memory_space=pltpu.VMEM)],
        out_specs=pl.BlockSpec(memory_space=pltpu.VMEM),
        scratch_shapes=[
            pltpu.VMEM((8, TILE, WIDTH), BF16),
            pltpu.VMEM((8, 2, TILE, WIDTH), BF16),
            pltpu.VMEM((2, 4, TILE, BLOCK), F32),
            pltpu.VMEM((5, 2, 40, BLOCK), F32),
            pltpu.VMEM((5, 2, PIECE, BLOCK), F32),
            pltpu.VMEM((4, PIECE, BLOCK), F32),
            pltpu.VMEM((3, 8, PIECE, 128), BF16),
            pltpu.VMEM((3, 8, PIECE, 128), BF16),
            pltpu.VMEM((WIDTH, BLOCK), BF16),
            pltpu.VMEM((2, 4, 2, 4, PIECE, BLOCK), BF16),
            pltpu.VMEM((8, TILE, BLOCK), BF16),
            pltpu.VMEM((8, 2, 2, 160, BLOCK), BF16),
            pltpu.VMEM((160, BLOCK), F32),
            pltpu.VMEM((384, WIDTH), F32),
            pltpu.VMEM((4, 4, 8, 128), F32),
            dma((6,)), dma((6,)), dma((9,)), dma((9,)), dma((8,)), dma((8,)),
            dma((5, 2)), dma((5, 2)), dma((5, 2)), dma((5, 2)), dma((3,)), dma((3,)), dma((4,)), dma((4,)),
            dma((4, 9)), dma((4, 9)), dma((4, 9)), dma((4, 9)), dma((4, 8)), dma((4, 8)),
            dma((2, 12)), dma((2, 12)), dma((2, 8)), dma((2, 8)),
            dma((4, 3)), dma((4, 3)),
        ],
        compiler_params=pltpu.CompilerParams(
            collective_id=0, has_side_effects=True, vmem_limit_bytes=60 << 20
        ),
    )(blended)


def per_device(grad, momentum):
    new_momentum = momentum_decay * momentum + grad
    blended = (grad + momentum_decay * new_momentum).astype(BF16)
    return (iterate(blended), new_momentum)


def solution(mesh):
    placed = (P("row", "col"), P("row", "col"))
    return jax.shard_map(
        per_device,
        mesh=mesh,
        in_specs=placed,
        out_specs=(P("row", "col"), P("row", "col")),
        check_vma=False,
    )
```

```python
import math

import jax
import jax.numpy as jnp
from jax import lax
from jax.experimental import pallas as pl
from jax.experimental.pallas import tpu as pltpu
from jax.sharding import PartitionSpec as P

momentum_decay = 0.95
target_rms = 0.25
norm_epsilon = 1e-07
coef_linear = 3.4445
coef_cubic = -4.775
coef_quintic = 2.0315

MESH = pl.DeviceIdType.MESH
F32 = jnp.float32
BF16 = jnp.bfloat16

TILE = 320
BLOCK = 640
WIDTH = 1024
PIECE = 80


class Gather:
    def __init__(self, own, whole, some, rows, cut, p, b, right, left, pair, send, recv, across=0, cut_pair=None):
        def copy(n, src, dst, device):
            return pltpu.make_async_remote_copy(
                src, dst, send.at[n], recv.at[n], device_id=device, device_id_type=MESH
            )

        def on(n, p, b, first, size, device):
            place = some(p, b, first, size)
            return copy(n, place, place, device)

        lo, hi = lax.rem(p + 3, 4), lax.rem(p + 1, 4)
        opp = lax.rem(p + 2, 4)
        c = 1 - b
        own_place = whole(p, b)
        around = rows - across
        cut_pair = cut if cut_pair is None else cut_pair
        self.pair = copy(0, own, own_place, pair)
        self.right = copy(1, own, own_place, right)
        self.left = copy(2, own, own_place, left)
        self.right_pair = on(3, p, c, 0, around, right)
        self.left_pair = on(4, p, c, 0, around, left)
        self.on_right = on(5, lo, b, 0, cut, right)
        self.on_left = on(6, hi, b, cut, rows - cut, left)
        self.on_right_pair = on(7, lo, c, 0, cut_pair, right)
        self.on_left_pair = on(8, hi, c, cut_pair, around - cut_pair, left)
        self.all = [
            self.pair, self.right, self.left, self.right_pair, self.left_pair,
            self.on_right, self.on_left, self.on_right_pair, self.on_left_pair,
        ]
        self.across = []
        if across:
            self.across = [on(9 + k, q, b, around, across, pair) for k, q in enumerate((lo, hi, opp))]
            self.all = self.all + self.across
        self.order = [(p, b), (p, c), (lo, b), (hi, b), (lo, c), (hi, c), (opp, b), (opp, c)]

    def start(self):
        self.pair.start()
        self.right.start()
        self.left.start()

    def arrive(self, n):
        waits = {
            1: [self.pair], 2: [self.right], 3: [self.left], 4: [self.right_pair], 5: [self.left_pair],
            6: [self.on_right, self.on_left], 7: [self.on_right_pair, self.on_left_pair],
        }
        starts = {
            1: [self.right_pair, self.left_pair], 2: [self.on_right], 3: [self.on_left],
            4: [self.on_right_pair], 5: [self.on_left_pair],
        }
        if self.across:
            for block, k in ((2, 0), (3, 1), (6, 2)):
                starts[block] = starts.get(block, []) + [self.across[k]]
        for c in waits[n]:
            c.wait_recv()
        for c in starts.get(n, []):
            c.start()

    def arrive_across(self, n):
        if self.across:
            self.across[{4: 0, 5: 1, 7: 2}[n]].wait_recv()

    def finish(self):
        for c in self.all:
            c.wait_send()


def kernel(
    blended, out,
    raw, ortho, part, hop_half, hop_whole, hop_pair, turned, turned_in, spots, gram_cols, gram_rows, poly, square, total, sums,
    b_send, b_recv, l_send, l_recv, bs_send, bs_recv, half_send, half_recv, whole_send, whole_recv, t_send, t_recv, z_send, z_recv,
    gr_send, gr_recv, gc_send, gc_recv, gs_send, gs_recv, p_send, p_recv, ps_send, ps_recv,
    sum_send, sum_recv,
):
    row, col = lax.axis_index("row"), lax.axis_index("col")
    core = lax.rem(row, 2)
    x = lax.rem(lax.div(row, 2), 4)
    z_lo = lax.div(row, 8)
    y, z_hi = lax.div(col, 2), lax.rem(col, 2)
    chip_row = lax.div(row, 2)

    def at(x=x, y=y, z_lo=z_lo, z_hi=z_hi, core=core):
        return ((z_lo * 4 + x) * 2 + core, y * 2 + z_hi)

    def turn(v, n):
        return lax.rem(v + n, 4)

    sibling = at(core=1 - core)
    x_right, x_left = at(x=turn(x, 1)), at(x=turn(x, 3))
    y_right, y_left = at(y=turn(y, 1)), at(y=turn(y, 3))
    lo_pair, hi_pair = at(z_lo=1 - z_lo), at(z_hi=1 - z_hi)
    z = z_hi * 2 + z_lo
    peers = {
        "core": [sibling],
        "x": [at(x=turn(x, n)) for n in (1, 2, 3)],
        "z": [at(z_lo=lax.rem(turn(z, n), 2), z_hi=lax.div(turn(z, n), 2)) for n in (1, 2, 3)],
        "y": [at(y=turn(y, n)) for n in (1, 2, 3)],
    }
    everyone = [d for group in peers.values() for d in group]

    barrier = pltpu.get_barrier_semaphore()
    for d in everyone:
        pl.semaphore_signal(barrier, inc=1, device_id=d, device_id_type=MESH)
    pl.semaphore_wait(barrier, len(everyone))

    lo, hi, opp = turn(x, 3), turn(x, 1), turn(x, 2)
    high = lax.div(x, 2)
    to_opp = high * z_lo + (1 - high) * (1 - z_lo)
    from_opp = (1 - high) * z_lo + high * (1 - z_lo)

    def b_copy(n, b, device, first=0, rows=TILE):
        place = raw.at[b * 4 + x, pl.ds(first, rows)]
        return pltpu.make_async_remote_copy(
            place, place, b_send.at[n], b_recv.at[n], device_id=device, device_id_type=MESH
        )

    across = [b_copy(0, z_lo, lo_pair, 0, 128), b_copy(1, z_lo, lo_pair, 128, 192)]
    own_left = b_copy(2, z_lo, x_left)
    other_right = [b_copy(3, 1 - z_lo, x_right, 0, 128), b_copy(4, 1 - z_lo, x_right, 128, 192)]
    first_opp = b_copy(5, to_opp, at(x=opp))
    order = [
        (x, z_lo), (x, 1 - z_lo), (hi, z_lo), (lo, 1 - z_lo), (opp, from_opp),
        (hi, 1 - z_lo), (lo, z_lo), (opp, 1 - from_opp),
    ]
    raw[z_lo * 4 + x] = blended[...]
    across[0].start()

    mine = jnp.zeros((8, 128), F32)
    for k in range(8):
        wide = blended[:, k * 128 : (k + 1) * 128].astype(F32).reshape(TILE // 8, 8, 128)
        mine = mine + jnp.sum(wide * wide, axis=0)
    for stage, (place, size) in enumerate(((core, 2), (x, 4), (z, 4), (y, 4))):
        group = list(peers.values())[stage]
        sums[stage, place] = mine
        copies = [
            pltpu.make_async_remote_copy(
                sums.at[stage, place], sums.at[stage, place],
                sum_send.at[stage, n], sum_recv.at[stage, n], device_id=d, device_id_type=MESH,
            )
            for n, d in enumerate(group)
        ]
        for c in copies:
            c.start()
        for c in copies:
            c.wait()
        mine = sums[stage, 0]
        for n in range(1, size):
            mine = mine + sums[stage, n]
        if stage == 1:
            own_left.start()
            pl.when(high == 1)(first_opp.start)
        elif stage == 2:
            across[1].start()
            across[0].wait_recv()
            other_right[0].start()
    squares_total = jnp.sum(mine, keepdims=True)
    norm_scale = target_rms * math.sqrt(5120) / (jnp.sqrt(squares_total) + norm_epsilon)

    def to_sibling(n, src, send, recv):
        return pltpu.make_async_remote_copy(
            src, src, send.at[n], recv.at[n], device_id=sibling, device_id_type=MESH
        )

    mine_rows = pl.ds(pl.multiple_of(y * PIECE, PIECE), PIECE)

    def scale(src, j):
        def body(k, carry):
            rows = pl.ds(pl.multiple_of(k * 32, 32), 32)
            ortho[j, core, rows] = (src[rows].astype(F32) * norm_scale).astype(BF16)
            return carry

        lax.fori_loop(0, TILE // 32, body, 0)

    def partial(p, b):
        part[b, p] = lax.dot_general(
            ortho[b * 4 + p, core],
            ortho[chip_row].reshape(BLOCK, WIDTH),
            (((1,), (1,)), ((), ())),
            preferred_element_type=F32,
        )

    def half_hops(n, p, b):
        far = turn(y, 2) * PIECE
        return [
            pltpu.make_async_remote_copy(
                part.at[b, p, pl.ds(pl.multiple_of(far + 40 * k, 8), 40)],
                hop_half.at[n, k],
                half_send.at[n, k], half_recv.at[n, k], device_id=d, device_id_type=MESH,
            )
            for k, d in enumerate((y_right, y_left))
        ]

    def whole_hops(n, p, b):
        return [
            pltpu.make_async_remote_copy(
                part.at[b, p, pl.ds(pl.multiple_of(near * PIECE, 8), PIECE)],
                hop_whole.at[n, k],
                whole_send.at[n, k], whole_recv.at[n, k], device_id=d, device_id_type=MESH,
            )
            for k, (near, d) in enumerate(((turn(y, 1), y_right), (turn(y, 3), y_left)))
        ]

    places = (x, lo, hi, opp)

    planes = (None, 1 - z_lo, z_lo, from_opp)

    tasks = ((x, z_lo), (x, 1 - z_lo), (lo, 1 - z_lo), (hi, z_lo), (opp, from_opp))

    def reduce_1(t):
        partial(*tasks[t])
        for c in half_hops(t, *tasks[t]):
            c.start()

    def reduce_2(t):
        p, b = tasks[t]
        halves, wholes = half_hops(t, p, b), whole_hops(t, p, b)
        for k, near in enumerate((turn(y, 1), turn(y, 3))):
            halves[k].wait_recv()
            rows = pl.ds(pl.multiple_of(near * PIECE + 40 * k, 8), 40)
            part[b, p, rows] = part[b, p, rows] + hop_half[t, k]
            wholes[k].start()

    def reduce_3(t):
        p, b = tasks[t]
        for c in whole_hops(t, p, b):
            c.wait_recv()
        part[b, p, mine_rows] = part[b, p, mine_rows] + (hop_whole[t, 0] + hop_whole[t, 1])

    def pair_hop(m):
        b = 1 - z_hi if m == 0 else planes[m]
        return pltpu.make_async_remote_copy(
            part.at[b, places[m], mine_rows], hop_pair.at[m],
            z_send.at[m], z_recv.at[m], device_id=hi_pair, device_id_type=MESH,
        )

    def reduce_4(m):
        if m == 0:
            pair_hop(0).start()
        else:
            pl.when(planes[m] != z_hi)(lambda: pair_hop(m).start())

    def keep(m, tile):
        p = places[m]
        gram_cols[z_hi, p, core, y] = tile
        gram_rows[chip_row, pl.ds(pl.multiple_of(p * PIECE, 16), PIECE)] = tile

    def summed(m):
        pair_hop(m).wait_recv()
        return part[z_hi, places[m], mine_rows] + hop_pair[m]

    def turned_pieces(m):
        away = (0, 2, 1, 3)[m]
        return [
            pltpu.make_async_remote_copy(
                turned.at[m - 1, a * 4 + k], turned_in.at[away - 1, core * 4 + y],
                t_send.at[m - 1], t_recv.at[away - 1],
                device_id=((z_hi * 4 + places[m]) * 2 + a, k * 2 + z_lo), device_id_type=MESH,
            )
            for a in range(2) for k in range(4)
        ]

    def all_turned(m):
        return pltpu.make_async_remote_copy(
            turned.at[m - 1], turned_in.at[m - 1],
            t_send.at[m - 1], t_recv.at[m - 1], device_id=sibling, device_id_type=MESH,
        )

    def reduce_5(m):
        @pl.when(planes[m] == z_hi)
        def _():
            tile = summed(m)
            keep(m, tile.astype(BF16))
            tall = jnp.concatenate([tile, jnp.zeros((128 - PIECE, BLOCK), F32)], axis=0).T
            turned[m - 1] = tall.astype(BF16).reshape(8, PIECE, 128)
            for c in turned_pieces(m):
                c.start()

    def finish_tile(m):
        if m == 0:
            keep(0, summed(0).astype(BF16))
            return

        @pl.when(planes[m] != z_hi)
        def _():
            all_turned(m).wait_recv()
            wide = jnp.concatenate([turned_in[m - 1, k] for k in range(8)], axis=1)
            keep(m, jnp.dot(wide, spots[...], preferred_element_type=F32).astype(BF16))

    def from_sibling(n):
        p, b = order[n]
        return to_sibling(n, ortho.at[b * 4 + p, core], bs_send, bs_recv)

    def later(k):
        if k == 8:
            place = ortho.at[(1 - to_opp) * 4 + x, core]
            return pltpu.make_async_remote_copy(
                place, place, l_send.at[8], l_recv.at[8], device_id=at(x=opp), device_id_type=MESH
            )
        p, b = (x, 1 - z_lo if k < 4 else z_lo)
        place = ortho.at[b * 4 + p, core, pl.ds(k % 4 * 80, 80)]
        return pltpu.make_async_remote_copy(
            place, place, l_send.at[k], l_recv.at[k],
                device_id=x_left if k < 4 else x_right, device_id_type=MESH
        )

    def process(n):
        p, b = order[n]
        scale(raw.at[b * 4 + p], b * 4 + p)
        from_sibling(n).start()
        if n == 0:
            from_sibling(0).wait_recv()

    def gather_rows(m):
        def place(p, b, first, rows):
            part_of = turn(p, (0, 3, 1, 2)[m]) * PIECE
            return gram_rows.at[b * 4 + p, pl.ds(pl.multiple_of(part_of + first, 16), rows)]

        return Gather(
            place(x, z_lo, 0, PIECE), lambda p, b: place(p, b, 0, PIECE), place,
            PIECE, 48, x, z_lo, x_right, x_left, lo_pair, gr_send.at[m], gr_recv.at[m],
        )

    def gather_cols(m):
        q = turn(x, (0, 3, 1, 2)[m])

        def place(p, b, first, rows):
            return gram_cols.at[b, q, core, p, pl.ds(first, rows)]

        return Gather(
            place(y, z_hi, 0, PIECE), lambda p, b: place(p, b, 0, PIECE), place,
            PIECE, 48, y, z_hi, y_right, y_left, hi_pair, gc_send.at[m], gc_recv.at[m],
        )

    def cols_to_sibling(m, n):
        p, b = cols_gathers[m].order[n]
        place = gram_cols.at[b, turn(x, (0, 3, 1, 2)[m]), core, p]
        return to_sibling(n, place, gs_send.at[m], gs_recv.at[m])

    rows_gathers = [gather_rows(m) for m in range(4)]
    cols_gathers = [gather_cols(m) for m in range(4)]

    def spread(m, event):
        if event == 0:
            finish_tile(m)
            cols_gathers[m].start()
            rows_gathers[m].start()
            cols_to_sibling(m, 0).start()
        for n in ((), (1, 2, 3), (4, 5), (6, 7))[event]:
            cols_gathers[m].arrive(n)
            cols_to_sibling(m, n).start()
            rows_gathers[m].arrive(n)

    spot = lax.broadcasted_iota(jnp.int32, (WIDTH, BLOCK), 0)
    column = lax.broadcasted_iota(jnp.int32, (WIDTH, BLOCK), 1)
    lane = spot % 128
    spots[...] = jnp.where((lane < PIECE) & (column == spot // 128 * PIECE + lane), 1.0, 0.0).astype(BF16)

    process(0)
    reduce_1(0)
    across[1].wait_recv()
    other_right[1].start()
    pl.when(high == 0)(first_opp.start)
    process(1)
    reduce_1(1)
    reduce_2(0)
    own_left.wait_recv()
    process(2)
    reduce_1(3)
    reduce_2(1)
    reduce_3(0)
    reduce_2(3)
    reduce_3(1)
    reduce_4(0)
    for c in other_right:
        c.wait_recv()
    process(3)
    reduce_1(2)
    later(0).start()
    later(4).start()
    reduce_3(3)
    reduce_4(2)
    later(1).start()
    later(5).start()
    first_opp.wait_recv()
    process(4)
    reduce_1(4)
    spread(0, 0)
    reduce_2(2)
    reduce_5(2)
    reduce_2(4)
    later(2).start()
    later(6).start()
    spread(0, 1)
    later(3).start()
    later(7).start()
    reduce_3(2)
    reduce_4(1)
    reduce_3(4)
    reduce_4(3)
    spread(0, 2)
    reduce_5(1)
    spread(1, 0)
    reduce_5(3)
    spread(2, 0)
    spread(0, 3)
    spread(1, 1)
    spread(3, 0)
    spread(2, 1)
    spread(1, 2)
    spread(3, 1)
    spread(2, 2)
    spread(3, 2)
    spread(1, 3)
    spread(2, 3)
    spread(3, 3)
    later(8).start()
    for m in range(4):
        for n in range(8):
            cols_to_sibling(m, n).wait_recv()

    def half_of_poly(h):
        rows = pl.ds(h * 160, 160)
        square[...] = jnp.zeros_like(square)

        def add_square(k, carry):
            right = gram_cols[lax.div(k, 4), lax.rem(k, 4)].reshape(BLOCK, BLOCK)
            square[...] += jnp.dot(gram_rows[k, rows], right, preferred_element_type=F32)
            return carry

        lax.fori_loop(0, 8, add_square, 0)
        poly[col, h, core] = (
            coef_cubic * gram_rows[chip_row, rows].astype(F32) + coef_quintic * square[...]
        ).astype(BF16)

    gathers_p = [
        Gather(
            poly.at[col, h, core],
            lambda p, b, h=h: poly.at[p * 2 + b, h, core],
            lambda p, b, first, rows, h=h: poly.at[p * 2 + b, h, core, pl.ds(first, rows)],
            160, 80, y, z_hi, y_right, y_left, hi_pair, p_send.at[h], p_recv.at[h], across=64, cut_pair=48,
        )
        for h in range(2)
    ]

    def poly_to_sibling(h, n):
        p, b = gathers_p[h].order[n]
        return to_sibling(n, poly.at[p * 2 + b, h, core], ps_send.at[h], ps_recv.at[h])

    for h in range(2):
        half_of_poly(h)
        gathers_p[h].start()
        poly_to_sibling(h, 0).start()

    lanes = pl.ds(pl.multiple_of(core * 256, 128), 384)
    total[...] = jnp.zeros_like(total)

    def add_product(n, columns):
        p, b = gathers_p[0].order[n]
        first = pl.multiple_of(p * PIECE, 16)
        left = [
            poly[p * 2 + b, lax.div(q, 2), a, pl.ds(pl.multiple_of(lax.rem(q, 2) * PIECE, 16), PIECE), lanes]
            for q in columns for a in range(2)
        ]
        right = [ortho[b * 4 + q, a, pl.ds(first, PIECE)] for q in columns for a in range(2)]
        total[...] += lax.dot_general(
            jnp.concatenate(left, axis=0), jnp.concatenate(right, axis=0),
            (((0,), (0,)), ((), ())), preferred_element_type=F32,
        )

    near, far = (x, hi), (lo, opp)

    for h in range(2):
        for n in (1, 2, 3):
            gathers_p[h].arrive(n)
            poly_to_sibling(h, n).start()
    for k in range(8):
        later(k).wait_recv()
        if k % 4 == 3:
            from_sibling(5 + k // 4).start()
    for n in range(1, 7):
        from_sibling(n).wait_recv()
    for n in range(4):
        for h in range(2):
            poly_to_sibling(h, n).wait_recv()
        add_product(n, near)
    for h in range(2):
        gathers_p[h].arrive(6)
        poly_to_sibling(h, 6).start()
        for n in (4, 5):
            gathers_p[h].arrive(n)
    later(8).wait_recv()
    from_sibling(7).start()
    for h in range(2):
        for n in (4, 5):
            gathers_p[h].arrive_across(n)
            poly_to_sibling(h, n).start()
    for n in (4, 5, 6):
        for h in range(2):
            poly_to_sibling(h, n).wait_recv()
        add_product(n, near)
    from_sibling(7).wait_recv()
    for n in range(7):
        add_product(n, far)
    for h in range(2):
        gathers_p[h].arrive(7)
        gathers_p[h].arrive_across(7)
        poly_to_sibling(h, 7).start()
    for h in range(2):
        poly_to_sibling(h, 7).wait_recv()
    add_product(7, near)
    add_product(7, far)

    product = total[pl.ds(pl.multiple_of(core * 64, 8), TILE)]
    out[...] = (
        math.sqrt(8192) * (coef_linear * ortho[chip_row, core].astype(F32) + product)
    ).astype(BF16)

    for c in across + other_right + [own_left, first_opp] + [later(k) for k in range(9)]:
        c.wait_send()
    for h in range(2):
        gathers_p[h].finish()
        for n in range(8):
            poly_to_sibling(h, n).wait_send()
    for n in range(8):
        from_sibling(n).wait_send()
    for t in range(5):
        for c in half_hops(t, *tasks[t]) + whole_hops(t, *tasks[t]):
            c.wait_send()
    pair_hop(0).wait_send()
    for m in (1, 2, 3):
        pl.when(planes[m] != z_hi)(lambda m=m: pair_hop(m).wait_send())
        pl.when(planes[m] == z_hi)(lambda m=m: all_turned(m).wait_send())
    for m in range(4):
        rows_gathers[m].finish()
        cols_gathers[m].finish()
        for n in range(8):
            cols_to_sibling(m, n).wait_send()


def iterate(blended):
    dma = pltpu.SemaphoreType.DMA
    return pl.pallas_call(
        kernel,
        out_shape=jax.ShapeDtypeStruct((TILE, WIDTH), BF16),
        in_specs=[pl.BlockSpec(memory_space=pltpu.VMEM)],
        out_specs=pl.BlockSpec(memory_space=pltpu.VMEM),
        scratch_shapes=[
            pltpu.VMEM((8, TILE, WIDTH), BF16),
            pltpu.VMEM((8, 2, TILE, WIDTH), BF16),
            pltpu.VMEM((2, 4, TILE, BLOCK), F32),
            pltpu.VMEM((5, 2, 40, BLOCK), F32),
            pltpu.VMEM((5, 2, PIECE, BLOCK), F32),
            pltpu.VMEM((4, PIECE, BLOCK), F32),
            pltpu.VMEM((3, 8, PIECE, 128), BF16),
            pltpu.VMEM((3, 8, PIECE, 128), BF16),
            pltpu.VMEM((WIDTH, BLOCK), BF16),
            pltpu.VMEM((2, 4, 2, 4, PIECE, BLOCK), BF16),
            pltpu.VMEM((8, TILE, BLOCK), BF16),
            pltpu.VMEM((8, 2, 2, 160, BLOCK), BF16),
            pltpu.VMEM((160, BLOCK), F32),
            pltpu.VMEM((384, WIDTH), F32),
            pltpu.VMEM((4, 4, 8, 128), F32),
            dma((6,)), dma((6,)), dma((9,)), dma((9,)), dma((8,)), dma((8,)),
            dma((5, 2)), dma((5, 2)), dma((5, 2)), dma((5, 2)), dma((3,)), dma((3,)), dma((4,)), dma((4,)),
            dma((4, 9)), dma((4, 9)), dma((4, 9)), dma((4, 9)), dma((4, 8)), dma((4, 8)),
            dma((2, 12)), dma((2, 12)), dma((2, 8)), dma((2, 8)),
            dma((4, 3)), dma((4, 3)),
        ],
        compiler_params=pltpu.CompilerParams(
            collective_id=0, has_side_effects=True, vmem_limit_bytes=60 << 20
        ),
    )(blended)


def per_device(grad, momentum):
    new_momentum = momentum_decay * momentum + grad
    blended = (grad + momentum_decay * new_momentum).astype(BF16)
    return (iterate(blended), new_momentum)


def solution(mesh):
    placed = (P("row", "col"), P("row", "col"))
    return jax.shard_map(
        per_device,
        mesh=mesh,
        in_specs=placed,
        out_specs=(P("row", "col"), P("row", "col")),
        check_vma=False,
    )
```
